32 devices in a mesh: groups: 2 (over y), gz: 4 (over z), gy: 2 (over x), af: 2 (over core).
Axes of the slice: x: 2, y: 2, z: 4, core: 2. Of those that a mesh axis runs over, the one named last changes fastest.
Arguments:
- atlas_features: bfloat16 [64, 256, 12, 128], P(('groups', 'gz'), ('gy', 'af')), parts along dimension 0, may hold values from -6 to 6
- velocity: bfloat16 [3, 64, 12, 128], P(None, ('groups', 'gz')), parts along dimension 1, may hold values from -0.25 to 0.25
- section_density: bfloat16 [64, 256, 1536], P(('groups', 'gz', 'gy', 'af')), parts along dimension 0, may hold values from -6 to 6
- pixel_mask: int32 [64, 1536], P(('groups', 'gz', 'gy', 'af')), parts along dimension 0, may hold values 0 or 1
- section_slice: int32 [64], P(('groups', 'gz')), parts along dimension 0, may hold values from 0 to 31, as said below
Outputs:
- feature_gradient: bfloat16 [64, 256, 12, 128], P(('groups', 'gz'), ('gy', 'af')), parts along dimension 0
The draws below stay inside these ranges and needn't reach their ends.
There are 2 independent parts, one for each index of `groups`. The reference program is written for one: setup_inputs(seed, part) draws one part's arguments, and reference() takes and returns one part's arrays. A program takes and returns all parts, laid end to end along the dimension named above; each array names one. Nothing has to cross between parts.
Inputs may be any that keep to these rules, and one draw needn't show every extreme that they name: `section_slice`: sections 8 * g to 8 * g + 7 match the slices 8 * g to 8 * g + 7, each once, in some order.
All inputs are finite; a program needn't handle non-finite values. No bound on the sum of `pixel_mask` on one device may be relied on, other than what follows from the above.
Results may differ from the reference program's by a relative error of at most 0.0096.
Values may be sent and summed in bfloat16 or wider, within the bound.
No kernel may reach another device: no remote copies, remote signals or barrier semaphores. Data moves between devices by JAX's collectives and lax.ppermute only.
A program may use at most 64 MiB of HBM per device.

```python
import jax
import jax.numpy as jnp
from jax import lax

C = 256
Q = 256
NX = 128
NY = 12
TSTEPS = 4
CZ = 8
NZ = 32


def draw_atlas_features(key, part):
    key = jax.random.fold_in(key, 11)
    array_shape = (NZ, C, NY, NX)
    values = jnp.clip(jax.random.normal(key, array_shape, jnp.float32), -6.0, 6.0)
    return values.astype(jnp.bfloat16)


def draw_section_slice(key, part):
    key = jax.random.fold_in(key, 23)
    blocks = NZ // CZ
    block_keys = jax.random.split(key, blocks)
    orders = jax.vmap(lambda one_key: jax.random.permutation(one_key, CZ))(block_keys)
    starts = (jnp.arange(blocks, dtype=jnp.int32) * CZ)[:, None]
    return (orders.astype(jnp.int32) + starts).reshape(NZ)


def place_ends(entries, key, least, high):
    shape = entries.shape
    index_at = [jax.random.randint(jax.random.fold_in(key, axis), (), 0, shape[axis]) for axis in range(len(shape))]
    entries = entries.at[tuple(index_at)].set(least)
    longest = shape.index(max(shape))
    index_at[longest] = (index_at[longest] + 1) % shape[longest]
    return entries.at[tuple(index_at)].set(high)


def levels(key, shape, cuts, low, largest):
    level = 1.0
    for position, parts in cuts:
        heights = jax.random.uniform(jax.random.fold_in(jax.random.fold_in(key, 6), position), (parts,), jnp.float32, low / len(cuts), largest / len(cuts))
        level = level * jnp.repeat(jnp.exp(heights), shape[position] // parts).reshape((-1,) + (1,) * (len(shape) - 1 - position))
    return level


def gaussian(own_key, shape, deviation, limit, pieces=(), kind=jnp.bfloat16):
    array = jax.random.normal(own_key, shape, jnp.float32) * deviation
    if len(pieces) > 0:
        array = levels(own_key, shape, pieces, -0.22, 0.18) * array
    return jnp.clip(array, min=-limit, max=limit).astype(kind)


def setup_inputs(seed: int = 0, part: int = 0) -> dict:
    key_list = jax.random.split(jax.random.key(seed), 6)
    part_keys = jax.random.split(jax.random.fold_in(key_list[5], part), 6)
    atlas_features = draw_atlas_features(jax.random.fold_in(jax.random.fold_in(key_list[5], part), 71), part)
    velocity = jnp.clip(jax.random.uniform(part_keys[1], (3, NZ, NY, NX), jnp.float32, -0.25, 0.25) * levels(part_keys[1], (3, NZ, NY, NX), ((1, 4),), -0.4, 0.0), -0.25, 0.25).astype(jnp.bfloat16)
    section_density = gaussian(part_keys[2], (NZ, Q, NY * NX), 1.0, 6.0, ((0, 16),))
    pixel_mask = place_ends((jax.random.randint(part_keys[3], (NZ, NY * NX), 0, 4) < 3).astype(jnp.int32), jax.random.fold_in(part_keys[3], 1), 0, 1)
    section_slice = draw_section_slice(jax.random.fold_in(jax.random.fold_in(key_list[5], part), 71), part)
    return {"atlas_features": atlas_features, "velocity": velocity, "section_density": section_density, "pixel_mask": pixel_mask, "section_slice": section_slice}


rate_diffuse = 0.04
ridge_weight = 0.25

def advance(padded, velocity_field):
    center = padded[1:-1]
    below_cell = padded[:-2]
    above_cell = padded[2:]
    sideways = jnp.pad(center, ((0, 0), (0, 0), (1, 1), (1, 1)))
    row_below = sideways[:, :, :-2, 1:-1]
    row_above = sideways[:, :, 2:, 1:-1]
    col_below = sideways[:, :, 1:-1, :-2]
    col_above = sideways[:, :, 1:-1, 2:]
    along_z = velocity_field[0][:, None]
    along_y = velocity_field[1][:, None]
    along_x = velocity_field[2][:, None]
    transport_term = jnp.maximum(along_z, 0.0) * (center - below_cell) + jnp.minimum(along_z, 0.0) * (above_cell - center) + jnp.maximum(along_y, 0.0) * (center - row_below) + jnp.minimum(along_y, 0.0) * (row_above - center) + jnp.maximum(along_x, 0.0) * (center - col_below) + jnp.minimum(along_x, 0.0) * (col_above - center)
    diffusion_term = below_cell + above_cell + row_below + row_above + col_below + col_above - 6.0 * center
    return center - transport_term + rate_diffuse * diffusion_term

def fit_section(slice_panel, density, pixel_valid):
    pixels = slice_panel.shape[-1]
    valid_pixel = pixel_valid[None, :] > 0
    masked = jnp.where(valid_pixel, slice_panel, jnp.zeros_like(slice_panel))
    gram_matrix = lax.dot_general(masked.astype(jnp.float32), slice_panel.astype(jnp.float32), (((1,), (1,)), ((), ())), preferred_element_type=jnp.float32) / pixels
    gram_matrix = gram_matrix + ridge_weight * jnp.eye(slice_panel.shape[0], dtype=jnp.float32)
    right_side = lax.dot_general(masked.astype(jnp.float32), density.astype(jnp.float32), (((1,), (1,)), ((), ())), preferred_element_type=jnp.float32) / pixels
    lower_factor = lax.linalg.cholesky(gram_matrix)
    halfway = lax.linalg.triangular_solve(lower_factor, right_side, left_side=True, lower=True)
    coefficient = lax.linalg.triangular_solve(lower_factor, halfway, left_side=True, lower=True, transpose_a=True)
    coefficient_low = coefficient.astype(jnp.bfloat16)
    fitted = lax.dot_general(coefficient_low.astype(jnp.float32), slice_panel.astype(jnp.float32), (((0,), (0,)), ((), ())), preferred_element_type=jnp.float32)
    residual = (fitted - density.astype(jnp.float32)).astype(jnp.bfloat16)
    pushed = jnp.dot(coefficient_low.astype(jnp.float32), residual.astype(jnp.float32), preferred_element_type=jnp.float32)
    return jnp.where(valid_pixel, 2.0 * pushed, 0.0).astype(jnp.bfloat16)

def reference(atlas_features, velocity, section_density, pixel_mask, section_slice):
    state_field = atlas_features.astype(jnp.float32)
    velocity_field = velocity.astype(jnp.float32)
    zero_row = jnp.zeros((1,) + state_field.shape[1:], jnp.float32)
    for repeat in range(TSTEPS):
        padded = jnp.concatenate([zero_row, state_field, zero_row], axis=0)
        state_field = advance(padded, velocity_field)
    moved_panel = state_field.astype(jnp.bfloat16).reshape(NZ, C, NY * NX)

    def one_section(inputs):
        slice_number, density, pixel_valid = inputs
        slice_panel = lax.dynamic_index_in_dim(moved_panel, slice_number, 0, keepdims=False)
        return fit_section(slice_panel, density, pixel_valid)
    gradients = lax.map(one_section, (section_slice, section_density, pixel_mask))
    result = jnp.zeros((NZ, C, NY * NX), jnp.bfloat16).at[section_slice].set(gradients)
    return result.reshape(NZ, C, NY, NX)
```

```python
import functools

import jax
import jax.numpy as jnp
from jax import lax
from jax.experimental import pallas as pl
from jax.experimental.pallas import tpu as pltpu
from jax.sharding import PartitionSpec as P

TSTEPS = 4
RATE = 0.04
RIDGE = 0.25
LANES = 128
F32 = jnp.float32
BF16 = jnp.bfloat16
VEL_ROWS = 16
EASY = 1.08
FAIR = 3.8


def spec(memory_space):
    return pl.BlockSpec(memory_space=memory_space)


def params(mib):
    return pltpu.CompilerParams(vmem_limit_bytes=mib << 20)


def pack_kernel(width, chunks, atlas, vel, *refs):
    outs, (low_vel, high_vel, sems) = refs[: 2 * chunks], refs[2 * chunks :]
    rows = atlas.shape[0]
    copies = []
    for part in range(chunks):
        for side, first in ((0, 0), (1, rows - TSTEPS)):
            out = outs[2 * part + side]
            for step in range(TSTEPS):
                copies.append(
                    pltpu.make_async_copy(
                        atlas.at[first + step, :, pl.ds(part * width, width), :],
                        out.at[:, pl.ds(step * width, width), :],
                        sems.at[len(copies)],
                    )
                )
                copies[-1].start()
    ny = atlas.shape[1]
    slots = TSTEPS - 1
    for side, first, box in ((0, 0, low_vel), (1, rows - slots, high_vel)):
        parts = [vel[k, :, first : first + slots, :].astype(F32) for k in range(3)]
        parts.append(jnp.zeros((ny, VEL_ROWS - 3 * slots, LANES), F32))
        box[...] = jnp.concatenate(parts, axis=1).astype(BF16)
        copies.append(
            pltpu.make_async_copy(
                box, outs[side].at[:, pl.ds(TSTEPS * width, VEL_ROWS), :], sems.at[len(copies)]
            )
        )
        copies[-1].start()
    for copy in copies:
        copy.wait()


def pack(atlas, vel, width, chunks):
    ny = atlas.shape[1]
    shapes = []
    for part in range(chunks):
        rows = TSTEPS * width + (VEL_ROWS if part == 0 else 0)
        shapes += [jax.ShapeDtypeStruct((ny, rows, LANES), BF16)] * 2
    return pl.pallas_call(
        functools.partial(pack_kernel, width, chunks),
        out_shape=shapes,
        in_specs=[spec(pl.ANY), spec(pltpu.VMEM)],
        out_specs=[spec(pl.ANY)] * len(shapes),
        scratch_shapes=[
            pltpu.VMEM((ny, VEL_ROWS, LANES), BF16),
            pltpu.VMEM((ny, VEL_ROWS, LANES), BF16),
            pltpu.SemaphoreType.DMA((2 * chunks * TSTEPS + 2,)),
        ],
        compiler_params=params(8),
        name="pack_edges",
    )(atlas, vel)


def transport_kernel(peers, per, scalars, slots, atlas, vel, low, high, low_vel, high_vel, *refs):
    outs, (state, speed, coef) = refs[: peers * per], refs[peers * per :]
    rows, ny, width = atlas.shape[:3]
    deep = rows + 2 * TSTEPS
    edge = TSTEPS - 1
    has_low, has_high, me = scalars[0], scalars[1], scalars[2]

    for k in range(3):
        speed[k, :, TSTEPS : TSTEPS + rows, :] = vel[k].astype(F32)
        below = low_vel[...].astype(F32)[:, edge * k : edge * (k + 1), :]
        above = high_vel[...].astype(F32)[:, edge * k : edge * (k + 1), :]
        speed[k, :, 1:TSTEPS, :] = below
        speed[k, :, TSTEPS + rows : TSTEPS + rows + edge, :] = above
    place = lax.broadcasted_iota(jnp.int32, (1, deep, LANES), 1)
    lane = lax.broadcasted_iota(jnp.int32, (1, deep, LANES), 2)
    inside = ((place >= TSTEPS) | (has_low > 0)) & ((place < TSTEPS + rows) | (has_high > 0))
    inside = inside & (place > 0) & (place < deep - 1)
    for y in range(ny):
        total = jnp.zeros((1, deep, LANES), F32)
        for k in range(3):
            v = speed[k, y : y + 1]
            from_low = jnp.maximum(v, 0.0) + RATE
            from_high = RATE - jnp.minimum(v, 0.0)
            total = total + (from_low + from_high)
            if k == 2:
                from_low = jnp.where(lane == 0, 0.0, from_low)
                from_high = jnp.where(lane == LANES - 1, 0.0, from_high)
            coef[2 * k + 1, y : y + 1] = jnp.where(inside, from_low, 0.0)
            coef[2 * k + 2, y : y + 1] = jnp.where(inside, from_high, 0.0)
        coef[0, y : y + 1] = jnp.where(inside, 1.0 - total, 0.0)

    def load(z, carry):
        state[0, z + TSTEPS] = atlas[z].astype(F32)
        return carry

    lax.fori_loop(0, rows, load, 0)
    for step in range(TSTEPS):
        part = slice(step * width, (step + 1) * width)
        state[0, step] = low[:, part, :].astype(F32)
        state[0, step + TSTEPS + rows] = high[:, part, :].astype(F32)

    def advance(source, z, carry):
        target = 1 - source
        for y in range(ny):
            weight = [coef[i, y, pl.ds(z, 1), :] for i in range(7)]
            center = state[source, z, y]
            total = weight[0] * center
            total = total + weight[1] * state[source, z - 1, y]
            total = total + weight[2] * state[source, z + 1, y]
            if y > 0:
                total = total + weight[3] * state[source, z, y - 1]
            if y < ny - 1:
                total = total + weight[4] * state[source, z, y + 1]
            total = total + weight[5] * pltpu.roll(center, 1, axis=1)
            total = total + weight[6] * pltpu.roll(center, LANES - 1, axis=1)
            state[target, z, y] = total
        return carry

    for step in range(TSTEPS):
        lax.fori_loop(step + 1, deep - 1 - step, functools.partial(advance, step % 2), 0)

    for k in range(peers):
        for s in range(per):
            z = slots[(me ^ k) * per + s] + TSTEPS
            for y in range(ny):
                value = state[TSTEPS % 2, z, y].astype(BF16)
                outs[k * per + s][:, y * LANES : (y + 1) * LANES] = value


def transport(scalars, slots, atlas, vel, low, high, low0, high0, width, part, peers, per):
    rows, ny = atlas.shape[:2]
    deep = rows + 2 * TSTEPS
    pixels = ny * LANES
    halo = pl.BlockSpec((ny, TSTEPS * width, LANES), lambda i: (0, 0, 0))
    tail = pl.BlockSpec((ny, VEL_ROWS, LANES), lambda i: (0, TSTEPS * width // VEL_ROWS, 0))
    return pl.pallas_call(
        functools.partial(transport_kernel, peers, per),
        grid=(1,),
        out_shape=[jax.ShapeDtypeStruct((width, pixels), BF16)] * (peers * per),
        in_specs=[
            spec(pltpu.SMEM),
            spec(pltpu.SMEM),
            pl.BlockSpec((rows, ny, width, LANES), lambda i: (0, 0, part, 0)),
            pl.BlockSpec(vel.shape, lambda i: (0, 0, 0, 0)),
            halo,
            halo,
            tail,
            tail,
        ],
        out_specs=[pl.BlockSpec((width, pixels), lambda i: (0, 0))] * (peers * per),
        scratch_shapes=[
            pltpu.VMEM((2, deep, ny, width, LANES), F32),
            pltpu.VMEM((3, ny, deep, LANES), F32),
            pltpu.VMEM((7, ny, deep, LANES), F32),
        ],
        compiler_params=params(56),
        name="transport",
    )(scalars, slots, atlas, vel, low, high, low0, high0)


def dot(a, b):
    return jnp.dot(a, b, preferred_element_type=F32)


def dot_full(a, b):
    return jnp.dot(a, b, preferred_element_type=F32, precision=lax.Precision.HIGHEST)


def halves(value):
    high = value.astype(BF16)
    return high, (value - high.astype(F32)).astype(BF16)


def fit_kernel(parts, peers, mask, density, *refs):
    blocks = refs[: parts * peers]
    outs = refs[parts * peers : parts * peers + peers]
    panel, gram, right, inverse, answer = refs[parts * peers + peers :]
    width, pixels = blocks[0].shape
    channels = panel.shape[0]
    share = channels // peers
    ny = pixels // LANES
    for k in range(peers):
        for part in range(parts):
            first = k * share + part * width
            panel[first : first + width, :] = blocks[k * parts + part][...]
    valid = mask[0] > 0
    every = panel[...]
    maps = density[0]
    masked = jnp.where(valid, every, jnp.zeros_like(every))
    contract = (((1,), (1,)), ((), ()))
    row = lax.broadcasted_iota(jnp.int32, (channels, channels), 0)
    column = lax.broadcasted_iota(jnp.int32, (channels, channels), 1)
    same = row == column
    gram[...] = lax.dot_general(every, masked, contract, preferred_element_type=F32) * (
        1.0 / pixels
    ) + jnp.where(same, RIDGE, 0.0)
    right[...] = lax.dot_general(maps, masked, contract, preferred_element_type=F32) * (
        1.0 / pixels
    )
    sums = jnp.sum(jnp.abs(gram[...]), axis=0, keepdims=True)
    bound_row = jnp.max(sums, axis=1, keepdims=True)
    bound = jnp.max(sums)
    start = 2.0 / (RIDGE + bound_row)
    spread = (bound_row - RIDGE) / (bound_row + RIDGE)

    def narrowed(spread):
        square = spread * spread
        return square / (2.0 - square), 2.0 / (2.0 - square)

    def doubled(scale):
        low = inverse[...].astype(BF16)
        left = jnp.where(same, 1.0, 0.0) - dot(gram[...].astype(BF16), low)
        inverse[...] = scale * (inverse[...] + dot(low, left.astype(BF16)))

    def refined():
        high, rest = halves(answer[...])
        gram_high, gram_rest = halves(gram[...])
        product = dot(high, gram_high) + (dot(rest, gram_high) + dot(high, gram_rest))
        left = (right[...] - product).astype(BF16)
        answer[...] = answer[...] + dot(left, inverse[...].astype(BF16))

    @pl.when(bound <= FAIR)
    def _():
        spread1, scale1 = narrowed(spread)
        spread2, scale2 = narrowed(spread1)
        _, scale3 = narrowed(spread2)
        inverse[...] = scale1 * (
            jnp.where(same, 2.0 * start, 0.0) - (start * start) * gram[...]
        )
        doubled(scale2)

        @pl.when(bound > EASY)
        def _():
            doubled(scale3)

        answer[...] = dot(right[...].astype(BF16), inverse[...].astype(BF16))
        refined()
        refined()

        @pl.when(bound > EASY)
        def _():
            refined()

    @pl.when(bound > FAIR)
    def _():
        inverse[...] = jnp.where(same, start, 0.0)

        def step(spread):
            left = jnp.where(same, 2.0, 0.0) - dot_full(gram[...], inverse[...])
            inverse[...] = dot_full(inverse[...], left)
            return spread * spread

        lax.while_loop(lambda spread: spread > 1e-4, step, jnp.max(spread))
        answer[...] = dot_full(right[...], inverse[...])
        for _ in range(3):
            left = right[...] - dot_full(answer[...], gram[...])
            answer[...] = answer[...] + dot_full(left, inverse[...])

    coefficient_t = answer[...].astype(BF16)
    coefficient = answer[...].T.astype(BF16)
    fitted = dot(coefficient_t, panel[...])
    residual = (fitted - maps.astype(F32)).astype(BF16)
    pushed = dot(coefficient, residual)
    gradient = jnp.where(valid, 2.0 * pushed, 0.0).astype(BF16)
    for k in range(peers):
        for y in range(ny):
            outs[k][y] = gradient[k * share : (k + 1) * share, y * LANES : (y + 1) * LANES]


def fit(mask, density, section, blocks, parts, peers):
    width, pixels = blocks[0].shape
    channels = width * parts * peers
    classes = density.shape[1]
    ny = pixels // LANES
    whole = pl.BlockSpec((width, pixels), lambda i: (0, 0))
    out = (ny, channels // peers, LANES)
    return pl.pallas_call(
        functools.partial(fit_kernel, parts, peers),
        grid=(1,),
        out_shape=[jax.ShapeDtypeStruct(out, BF16)] * peers,
        in_specs=[
            pl.BlockSpec((1, 1, pixels), lambda i: (section, 0, 0)),
            pl.BlockSpec((1, classes, pixels), lambda i: (section, 0, 0)),
        ]
        + [whole] * len(blocks),
        out_specs=[pl.BlockSpec(out, lambda i: (0, 0, 0))] * peers,
        scratch_shapes=[
            pltpu.VMEM((channels, pixels), BF16),
            pltpu.VMEM((channels, channels), F32),
            pltpu.VMEM((classes, channels), F32),
            pltpu.VMEM((channels, channels), F32),
            pltpu.VMEM((classes, channels), F32),
        ],
        compiler_params=params(48),
        name="fit",
    )(mask, density, *blocks)


def place_kernel(peers, per, section, scalars, slots, *refs):
    blocks = refs[:peers]
    out, sems = refs[-2], refs[-1]
    me = scalars[2]
    copies = [
        pltpu.make_async_copy(
            blocks[k], out.at[slots[(me ^ k) * per + section]], sems.at[k]
        )
        for k in range(peers)
    ]
    for copy in copies:
        copy.start()
    for copy in copies:
        copy.wait()


def place(scalars, slots, blocks, earlier, rows, section, per):
    peers = len(blocks)
    extra = [] if earlier is None else [earlier]
    return pl.pallas_call(
        functools.partial(place_kernel, peers, per, section),
        out_shape=jax.ShapeDtypeStruct((rows,) + blocks[0].shape, BF16),
        in_specs=[spec(pltpu.SMEM)] * 2 + [spec(pl.ANY)] * (peers + len(extra)),
        out_specs=spec(pl.ANY),
        scratch_shapes=[pltpu.SemaphoreType.DMA((peers,))],
        input_output_aliases={2 + peers: 0} if extra else {},
        name="place",
    )(scalars, slots, *blocks, *extra)


def body(atlas_features, velocity, section_density, pixel_mask, section_slice):
    rows, channels = atlas_features.shape[:2]
    slabs = lax.axis_size("gz")
    slab = lax.axis_index("gz")
    peers = lax.axis_size(("gy", "af"))
    me = lax.axis_index(("gy", "af"))
    per = section_density.shape[0]
    chunks = 1
    width = channels // chunks

    atlas = jnp.transpose(atlas_features, (0, 2, 1, 3))
    vel = jnp.transpose(velocity, (0, 2, 1, 3))
    mask = pixel_mask.reshape(per, 1, -1)
    slots = section_slice - slab * rows
    scalars = jnp.stack([slab > 0, slab < slabs - 1, me]).astype(jnp.int32)

    edges = pack(atlas, vel, width, chunks)
    upward = [(i, i + 1) for i in range(slabs - 1)]
    downward = [(i + 1, i) for i in range(slabs - 1)]
    halos = []
    for part in range(chunks):
        low = lax.ppermute(edges[2 * part + 1], "gz", upward)
        high = lax.ppermute(edges[2 * part], "gz", downward)
        halos.append((low, high))

    def swap(block, k):
        if k == 0:
            return block
        return lax.ppermute(block, ("gy", "af"), [(i, i ^ k) for i in range(peers)])

    arrived = {}
    for part in range(chunks):
        moved = transport(
            scalars, slots, atlas, vel, *halos[part], *halos[0], width, part, peers, per
        )
        for s in range(per):
            for k in range(peers):
                arrived[s, k, part] = swap(moved[k * per + s], k)

    result = None
    for s in range(per):
        blocks = [arrived[s, k, part] for k in range(peers) for part in range(chunks)]
        gradients = fit(mask, section_density, s, blocks, chunks, peers)
        returned = [swap(gradients[k], k) for k in range(peers)]
        result = place(scalars, slots, returned, result, rows, s, per)
    return jnp.transpose(result, (0, 2, 1, 3))


def solution(mesh):
    return jax.shard_map(
        body,
        mesh=mesh,
        in_specs=(
            P(("groups", "gz"), ("gy", "af"), None, None),
            P(None, ("groups", "gz"), None, None),
            P(("groups", "gz", "gy", "af"), None, None),
            P(("groups", "gz", "gy", "af"), None),
            P(("groups", "gz")),
        ),
        out_specs=P(("groups", "gz"), ("gy", "af"), None, None),
        check_vma=False,
    )
```

```python
import functools

import jax
import jax.numpy as jnp
from jax import lax
from jax.experimental import pallas as pl
from jax.experimental.pallas import tpu as pltpu
from jax.sharding import PartitionSpec as P

TSTEPS = 4
RATE = 0.04
RIDGE = 0.25
LANES = 128
F32 = jnp.float32
BF16 = jnp.bfloat16
VEL_ROWS = 16
EASY = 1.08
FAIR = 3.8


def spec(memory_space):
    return pl.BlockSpec(memory_space=memory_space)


def params(mib):
    return pltpu.CompilerParams(vmem_limit_bytes=mib << 20)


def pack_kernel(width, chunks, atlas, vel, *refs):
    outs, (low_vel, high_vel, sems) = refs[: 2 * chunks], refs[2 * chunks :]
    rows = atlas.shape[0]
    copies = []
    for part in range(chunks):
        for side, first in ((0, 0), (1, rows - TSTEPS)):
            out = outs[2 * part + side]
            for step in range(TSTEPS):
                copies.append(
                    pltpu.make_async_copy(
                        atlas.at[first + step, :, pl.ds(part * width, width), :],
                        out.at[:, pl.ds(step * width, width), :],
                        sems.at[len(copies)],
                    )
                )
                copies[-1].start()
    ny = atlas.shape[1]
    slots = TSTEPS - 1
    for side, first, box in ((0, 0, low_vel), (1, rows - slots, high_vel)):
        parts = [vel[k, :, first : first + slots, :].astype(F32) for k in range(3)]
        parts.append(jnp.zeros((ny, VEL_ROWS - 3 * slots, LANES), F32))
        box[...] = jnp.concatenate(parts, axis=1).astype(BF16)
        copies.append(
            pltpu.make_async_copy(
                box, outs[side].at[:, pl.ds(TSTEPS * width, VEL_ROWS), :], sems.at[len(copies)]
            )
        )
        copies[-1].start()
    for copy in copies:
        copy.wait()


def pack(atlas, vel, width, chunks):
    ny = atlas.shape[1]
    shapes = []
    for part in range(chunks):
        rows = TSTEPS * width + (VEL_ROWS if part == 0 else 0)
        shapes += [jax.ShapeDtypeStruct((ny, rows, LANES), BF16)] * 2
    return pl.pallas_call(
        functools.partial(pack_kernel, width, chunks),
        out_shape=shapes,
        in_specs=[spec(pltpu.HBM), spec(pltpu.VMEM)],
        out_specs=[spec(pl.ANY)] * len(shapes),
        scratch_shapes=[
            pltpu.VMEM((ny, VEL_ROWS, LANES), BF16),
            pltpu.VMEM((ny, VEL_ROWS, LANES), BF16),
            pltpu.SemaphoreType.DMA((2 * chunks * TSTEPS + 2,)),
        ],
        compiler_params=params(8),
        name="pack_edges",
    )(atlas, vel)


def transport_kernel(peers, per, scalars, slots, atlas, vel, low, high, low_vel, high_vel, *refs):
    outs, (state, speed, coef) = refs[: peers * per], refs[peers * per :]
    rows, ny, width = atlas.shape[:3]
    deep = rows + 2 * TSTEPS
    edge = TSTEPS - 1
    has_low, has_high, me = scalars[0], scalars[1], scalars[2]

    for k in range(3):
        speed[k, :, TSTEPS : TSTEPS + rows, :] = vel[k].astype(F32)
        below = low_vel[...].astype(F32)[:, edge * k : edge * (k + 1), :]
        above = high_vel[...].astype(F32)[:, edge * k : edge * (k + 1), :]
        speed[k, :, 1:TSTEPS, :] = below
        speed[k, :, TSTEPS + rows : TSTEPS + rows + edge, :] = above
    place = lax.broadcasted_iota(jnp.int32, (1, deep, LANES), 1)
    lane = lax.broadcasted_iota(jnp.int32, (1, deep, LANES), 2)
    inside = ((place >= TSTEPS) | (has_low > 0)) & ((place < TSTEPS + rows) | (has_high > 0))
    inside = inside & (place > 0) & (place < deep - 1)
    for y in range(ny):
        total = jnp.zeros((1, deep, LANES), F32)
        for k in range(3):
            v = speed[k, y : y + 1]
            from_low = jnp.maximum(v, 0.0) + RATE
            from_high = RATE - jnp.minimum(v, 0.0)
            total = total + (from_low + from_high)
            if k == 2:
                from_low = jnp.where(lane == 0, 0.0, from_low)
                from_high = jnp.where(lane == LANES - 1, 0.0, from_high)
            coef[2 * k + 1, y : y + 1] = jnp.where(inside, from_low, 0.0)
            coef[2 * k + 2, y : y + 1] = jnp.where(inside, from_high, 0.0)
        coef[0, y : y + 1] = jnp.where(inside, 1.0 - total, 0.0)

    def load(z, carry):
        state[0, z + TSTEPS] = atlas[z].astype(F32)
        return carry

    lax.fori_loop(0, rows, load, 0)
    for step in range(TSTEPS):
        part = slice(step * width, (step + 1) * width)
        state[0, step] = low[:, part, :].astype(F32)
        state[0, step + TSTEPS + rows] = high[:, part, :].astype(F32)

    def advance(source, z, carry):
        target = 1 - source
        for y in range(ny):
            weight = [coef[i, y, pl.ds(z, 1), :] for i in range(7)]
            center = state[source, z, y]
            total = weight[0] * center
            total = total + weight[1] * state[source, z - 1, y]
            total = total + weight[2] * state[source, z + 1, y]
            if y > 0:
                total = total + weight[3] * state[source, z, y - 1]
            if y < ny - 1:
                total = total + weight[4] * state[source, z, y + 1]
            total = total + weight[5] * pltpu.roll(center, 1, axis=1)
            total = total + weight[6] * pltpu.roll(center, LANES - 1, axis=1)
            state[target, z, y] = total
        return carry

    for step in range(TSTEPS):
        lax.fori_loop(step + 1, deep - 1 - step, functools.partial(advance, step % 2), 0)

    for k in range(peers):
        for s in range(per):
            z = slots[(me ^ k) * per + s] + TSTEPS
            for y in range(ny):
                value = state[TSTEPS % 2, z, y].astype(BF16)
                outs[k * per + s][:, y * LANES : (y + 1) * LANES] = value


def transport(scalars, slots, atlas, vel, low, high, low0, high0, width, part, peers, per):
    rows, ny = atlas.shape[:2]
    deep = rows + 2 * TSTEPS
    pixels = ny * LANES
    halo = pl.BlockSpec((ny, TSTEPS * width, LANES), lambda i: (0, 0, 0))
    tail = pl.BlockSpec((ny, VEL_ROWS, LANES), lambda i: (0, TSTEPS * width // VEL_ROWS, 0))
    return pl.pallas_call(
        functools.partial(transport_kernel, peers, per),
        grid=(1,),
        out_shape=[jax.ShapeDtypeStruct((width, pixels), BF16)] * (peers * per),
        in_specs=[
            spec(pltpu.SMEM),
            spec(pltpu.SMEM),
            pl.BlockSpec((rows, ny, width, LANES), lambda i: (0, 0, part, 0)),
            pl.BlockSpec(vel.shape, lambda i: (0, 0, 0, 0)),
            halo,
            halo,
            tail,
            tail,
        ],
        out_specs=[pl.BlockSpec((width, pixels), lambda i: (0, 0))] * (peers * per),
        scratch_shapes=[
            pltpu.VMEM((2, deep, ny, width, LANES), F32),
            pltpu.VMEM((3, ny, deep, LANES), F32),
            pltpu.VMEM((7, ny, deep, LANES), F32),
        ],
        compiler_params=params(56),
        name="transport",
    )(scalars, slots, atlas, vel, low, high, low0, high0)


def dot(a, b):
    return jnp.dot(a, b, preferred_element_type=F32)


def dot_full(a, b):
    return jnp.dot(a, b, preferred_element_type=F32, precision=lax.Precision.HIGHEST)


def halves(value):
    high = value.astype(BF16)
    return high, (value - high.astype(F32)).astype(BF16)


def fit_kernel(parts, peers, mask, density, *refs):
    blocks = refs[: parts * peers]
    outs = refs[parts * peers : parts * peers + peers]
    panel, gram, right, inverse, answer = refs[parts * peers + peers :]
    width, pixels = blocks[0].shape
    channels = panel.shape[0]
    share = channels // peers
    ny = pixels // LANES
    for k in range(peers):
        for part in range(parts):
            first = k * share + part * width
            panel[first : first + width, :] = blocks[k * parts + part][...]
    valid = mask[0] > 0
    every = panel[...]
    maps = density[0]
    masked = jnp.where(valid, every, jnp.zeros_like(every))
    contract = (((1,), (1,)), ((), ()))
    row = lax.broadcasted_iota(jnp.int32, (channels, channels), 0)
    column = lax.broadcasted_iota(jnp.int32, (channels, channels), 1)
    same = row == column
    gram[...] = lax.dot_general(every, masked, contract, preferred_element_type=F32) * (
        1.0 / pixels
    ) + jnp.where(same, RIDGE, 0.0)
    right[...] = lax.dot_general(maps, masked, contract, preferred_element_type=F32) * (
        1.0 / pixels
    )
    sums = jnp.sum(jnp.abs(gram[...]), axis=0, keepdims=True)
    bound_row = jnp.max(sums, axis=1, keepdims=True)
    bound = jnp.max(sums)
    start = 2.0 / (RIDGE + bound_row)
    spread = (bound_row - RIDGE) / (bound_row + RIDGE)

    def narrowed(spread):
        square = spread * spread
        return square / (2.0 - square), 2.0 / (2.0 - square)

    def doubled(scale):
        low = inverse[...].astype(BF16)
        left = jnp.where(same, 1.0, 0.0) - dot(gram[...].astype(BF16), low)
        inverse[...] = scale * (inverse[...] + dot(low, left.astype(BF16)))

    def refined():
        high, rest = halves(answer[...])
        gram_high, gram_rest = halves(gram[...])
        product = dot(high, gram_high) + (dot(rest, gram_high) + dot(high, gram_rest))
        left = (right[...] - product).astype(BF16)
        answer[...] = answer[...] + dot(left, inverse[...].astype(BF16))

    @pl.when(bound <= FAIR)
    def _():
        spread1, scale1 = narrowed(spread)
        spread2, scale2 = narrowed(spread1)
        _, scale3 = narrowed(spread2)
        inverse[...] = scale1 * (
            jnp.where(same, 2.0 * start, 0.0) - (start * start) * gram[...]
        )
        doubled(scale2)

        @pl.when(bound > EASY)
        def _():
            doubled(scale3)

        answer[...] = dot(right[...].astype(BF16), inverse[...].astype(BF16))
        refined()
        refined()

        @pl.when(bound > EASY)
        def _():
            refined()

    @pl.when(bound > FAIR)
    def _():
        inverse[...] = jnp.where(same, start, 0.0)

        def step(spread):
            left = jnp.where(same, 2.0, 0.0) - dot_full(gram[...], inverse[...])
            inverse[...] = dot_full(inverse[...], left)
            return spread * spread

        lax.while_loop(lambda spread: spread > 1e-4, step, jnp.max(spread))
        answer[...] = dot_full(right[...], inverse[...])
        for _ in range(3):
            left = right[...] - dot_full(answer[...], gram[...])
            answer[...] = answer[...] + dot_full(left, inverse[...])

    coefficient_t = answer[...].astype(BF16)
    coefficient = answer[...].T.astype(BF16)
    fitted = dot(coefficient_t, panel[...])
    residual = (fitted - maps.astype(F32)).astype(BF16)
    pushed = dot(coefficient, residual)
    gradient = jnp.where(valid, 2.0 * pushed, 0.0).astype(BF16)
    for k in range(peers):
        for y in range(ny):
            outs[k][y] = gradient[k * share : (k + 1) * share, y * LANES : (y + 1) * LANES]


def fit(mask, density, section, blocks, parts, peers):
    width, pixels = blocks[0].shape
    channels = width * parts * peers
    classes = density.shape[1]
    ny = pixels // LANES
    whole = pl.BlockSpec((width, pixels), lambda i: (0, 0))
    out = (ny, channels // peers, LANES)
    return pl.pallas_call(
        functools.partial(fit_kernel, parts, peers),
        grid=(1,),
        out_shape=[jax.ShapeDtypeStruct(out, BF16)] * peers,
        in_specs=[
            pl.BlockSpec((1, 1, pixels), lambda i: (section, 0, 0)),
            pl.BlockSpec((1, classes, pixels), lambda i: (section, 0, 0)),
        ]
        + [whole] * len(blocks),
        out_specs=[pl.BlockSpec(out, lambda i: (0, 0, 0))] * peers,
        scratch_shapes=[
            pltpu.VMEM((channels, pixels), BF16),
            pltpu.VMEM((channels, channels), F32),
            pltpu.VMEM((classes, channels), F32),
            pltpu.VMEM((channels, channels), F32),
            pltpu.VMEM((classes, channels), F32),
        ],
        compiler_params=params(48),
        name="fit",
    )(mask, density, *blocks)


def place_kernel(peers, per, section, scalars, slots, *refs):
    blocks = refs[:peers]
    out, sems = refs[-2], refs[-1]
    me = scalars[2]
    copies = [
        pltpu.make_async_copy(
            blocks[k], out.at[slots[(me ^ k) * per + section]], sems.at[k]
        )
        for k in range(peers)
    ]
    for copy in copies:
        copy.start()
    for copy in copies:
        copy.wait()


def place(scalars, slots, blocks, earlier, rows, section, per):
    peers = len(blocks)
    extra = [] if earlier is None else [earlier]
    return pl.pallas_call(
        functools.partial(place_kernel, peers, per, section),
        out_shape=jax.ShapeDtypeStruct((rows,) + blocks[0].shape, BF16),
        in_specs=[spec(pltpu.SMEM)] * 2
        + [spec(pltpu.VMEM)] * peers
        + [spec(pl.ANY)] * len(extra),
        out_specs=spec(pl.ANY),
        scratch_shapes=[pltpu.SemaphoreType.DMA((peers,))],
        input_output_aliases={2 + peers: 0} if extra else {},
        compiler_params=params(16),
        name="place",
    )(scalars, slots, *blocks, *extra)


def body(atlas_features, velocity, section_density, pixel_mask, section_slice):
    rows, channels = atlas_features.shape[:2]
    slabs = lax.axis_size("gz")
    slab = lax.axis_index("gz")
    peers = lax.axis_size(("gy", "af"))
    me = lax.axis_index(("gy", "af"))
    per = section_density.shape[0]
    chunks = 1
    width = channels // chunks

    atlas = jnp.transpose(atlas_features, (0, 2, 1, 3))
    vel = jnp.transpose(velocity, (0, 2, 1, 3))
    mask = pixel_mask.reshape(per, 1, -1)
    slots = section_slice - slab * rows
    scalars = jnp.stack([slab > 0, slab < slabs - 1, me]).astype(jnp.int32)

    edges = pack(atlas, vel, width, chunks)
    upward = [(i, i + 1) for i in range(slabs - 1)]
    downward = [(i + 1, i) for i in range(slabs - 1)]
    halos = []
    for part in range(chunks):
        low = lax.ppermute(edges[2 * part + 1], "gz", upward)
        high = lax.ppermute(edges[2 * part], "gz", downward)
        halos.append((low, high))

    def swap(block, k):
        if k == 0:
            return block
        return lax.ppermute(block, ("gy", "af"), [(i, i ^ k) for i in range(peers)])

    arrived = {}
    for part in range(chunks):
        moved = transport(
            scalars, slots, atlas, vel, *halos[part], *halos[0], width, part, peers, per
        )
        for s in range(per):
            for k in range(peers):
                arrived[s, k, part] = swap(moved[k * per + s], k)

    result = None
    for s in range(per):
        blocks = [arrived[s, k, part] for k in range(peers) for part in range(chunks)]
        gradients = fit(mask, section_density, s, blocks, chunks, peers)
        returned = [swap(gradients[k], k) for k in range(peers)]
        result = place(scalars, slots, returned, result, rows, s, per)
    return jnp.transpose(result, (0, 2, 1, 3))


def solution(mesh):
    return jax.shard_map(
        body,
        mesh=mesh,
        in_specs=(
            P(("groups", "gz"), ("gy", "af"), None, None),
            P(None, ("groups", "gz"), None, None),
            P(("groups", "gz", "gy", "af"), None, None),
            P(("groups", "gz", "gy", "af"), None),
            P(("groups", "gz")),
        ),
        out_specs=P(("groups", "gz"), ("gy", "af"), None, None),
        check_vma=False,
    )
```

```python
import functools

import jax
import jax.numpy as jnp
from jax import lax
from jax.experimental import pallas as pl
from jax.experimental.pallas import tpu as pltpu
from jax.sharding import PartitionSpec as P

TSTEPS = 4
RATE = 0.04
RIDGE = 0.25
LANES = 128
F32 = jnp.float32
BF16 = jnp.bfloat16
VEL_ROWS = 16
CHUNK = 32
COST_T, COST_F, COST_P = 10 * 10**9, 3 * 10**9, 15 * 10**8
EASY = 1.08
FAIR = 3.8


def spec(memory_space):
    return pl.BlockSpec(memory_space=memory_space)


def cost(count):
    return pl.CostEstimate(flops=count, bytes_accessed=0, transcendentals=0)


def params(mib):
    return pltpu.CompilerParams(vmem_limit_bytes=mib << 20)


def pack_kernel(width, chunks, atlas, vel, *refs):
    outs, (low_vel, high_vel, sems) = refs[: 2 * chunks], refs[2 * chunks :]
    rows = atlas.shape[0]
    copies = []
    for part in range(chunks):
        for side, first in ((0, 0), (1, rows - TSTEPS)):
            out = outs[2 * part + side]
            for step in range(TSTEPS):
                copies.append(
                    pltpu.make_async_copy(
                        atlas.at[first + step, :, pl.ds(part * width, width), :],
                        out.at[:, pl.ds(step * width, width), :],
                        sems.at[len(copies)],
                    )
                )
                copies[-1].start()
    ny = atlas.shape[1]
    slots = TSTEPS - 1
    for side, first, box in ((0, 0, low_vel), (1, rows - slots, high_vel)):
        parts = [vel[k, :, first : first + slots, :].astype(F32) for k in range(3)]
        parts.append(jnp.zeros((ny, VEL_ROWS - 3 * slots, LANES), F32))
        box[...] = jnp.concatenate(parts, axis=1).astype(BF16)
        copies.append(
            pltpu.make_async_copy(
                box, outs[side].at[:, pl.ds(TSTEPS * width, VEL_ROWS), :], sems.at[len(copies)]
            )
        )
        copies[-1].start()
    for copy in copies:
        copy.wait()


def pack(atlas, vel, width, chunks):
    ny = atlas.shape[1]
    shapes = []
    for part in range(chunks):
        rows = TSTEPS * width + (VEL_ROWS if part == 0 else 0)
        shapes += [jax.ShapeDtypeStruct((ny, rows, LANES), BF16)] * 2
    return pl.pallas_call(
        functools.partial(pack_kernel, width, chunks),
        out_shape=shapes,
        in_specs=[spec(pltpu.HBM), spec(pltpu.VMEM)],
        out_specs=[spec(pl.ANY)] * len(shapes),
        scratch_shapes=[
            pltpu.VMEM((ny, VEL_ROWS, LANES), BF16),
            pltpu.VMEM((ny, VEL_ROWS, LANES), BF16),
            pltpu.SemaphoreType.DMA((2 * chunks * TSTEPS + 2,)),
        ],
        compiler_params=params(8),
        name="pack_edges",
    )(atlas, vel)


def transport_kernel(
    peers, per, joined, width, part, scalars, slots, atlas, vel, low, high, low0, high0, *refs
):
    outs, (state, speed, coef) = refs[:-3], refs[-3:]
    rows, ny = atlas.shape[:2]
    tail = slice(TSTEPS * width, TSTEPS * width + VEL_ROWS)
    deep = rows + 2 * TSTEPS
    edge = TSTEPS - 1
    has_low, has_high, me = scalars[0], scalars[1], scalars[2]

    for k in range(3):
        speed[k, :, TSTEPS : TSTEPS + rows, :] = vel[k].astype(F32)
        below = low0[:, tail, :].astype(F32)[:, edge * k : edge * (k + 1), :]
        above = high0[:, tail, :].astype(F32)[:, edge * k : edge * (k + 1), :]
        speed[k, :, 1:TSTEPS, :] = below
        speed[k, :, TSTEPS + rows : TSTEPS + rows + edge, :] = above
    place = lax.broadcasted_iota(jnp.int32, (1, deep, LANES), 1)
    lane = lax.broadcasted_iota(jnp.int32, (1, deep, LANES), 2)
    inside = ((place >= TSTEPS) | (has_low > 0)) & ((place < TSTEPS + rows) | (has_high > 0))
    inside = inside & (place > 0) & (place < deep - 1)
    for y in range(ny):
        total = jnp.zeros((1, deep, LANES), F32)
        for k in range(3):
            v = speed[k, y : y + 1]
            from_low = jnp.maximum(v, 0.0) + RATE
            from_high = RATE - jnp.minimum(v, 0.0)
            total = total + (from_low + from_high)
            if k == 2:
                from_low = jnp.where(lane == 0, 0.0, from_low)
                from_high = jnp.where(lane == LANES - 1, 0.0, from_high)
            coef[2 * k + 1, y : y + 1] = jnp.where(inside, from_low, 0.0)
            coef[2 * k + 2, y : y + 1] = jnp.where(inside, from_high, 0.0)
        coef[0, y : y + 1] = jnp.where(inside, 1.0 - total, 0.0)

    def load(z, carry):
        state[0, z + TSTEPS] = atlas[z, :, part * width : (part + 1) * width, :].astype(F32)
        return carry

    lax.fori_loop(0, rows, load, 0)
    for step in range(TSTEPS):
        span = slice(step * width, (step + 1) * width)
        state[0, step] = low[:, span, :].astype(F32)
        state[0, step + TSTEPS + rows] = high[:, span, :].astype(F32)

    def advance(source, z):
        target = 1 - source
        for y in range(ny):
            weight = [coef[i, y, pl.ds(z, 1), :] for i in range(7)]
            center = state[source, z, y]
            total = weight[0] * center
            total = total + weight[1] * state[source, z - 1, y]
            total = total + weight[2] * state[source, z + 1, y]
            if y > 0:
                total = total + weight[3] * state[source, z, y - 1]
            if y < ny - 1:
                total = total + weight[4] * state[source, z, y + 1]
            total = total + weight[5] * pltpu.roll(center, 1, axis=1)
            total = total + weight[6] * pltpu.roll(center, LANES - 1, axis=1)
            state[target, z, y] = total

    def two(source, first, i, carry):
        advance(source, first + 2 * i)
        advance(source, first + 2 * i + 1)
        return carry

    for step in range(TSTEPS):
        pairs = (deep - 2 * (step + 1)) // 2
        lax.fori_loop(0, pairs, functools.partial(two, step % 2, step + 1), 0)

    for k in range(peers):
        for s in range(per):
            z = slots[(me ^ k) * per + s] + TSTEPS
            out = outs[k].at[s] if joined else outs[k * per + s].at[0]
            for y in range(ny):
                value = state[TSTEPS % 2, z, y].astype(BF16)
                out[:, y * LANES : (y + 1) * LANES] = value


def transport(scalars, slots, atlas, vel, low, high, low0, high0, width, part, peers, per, joined):
    rows, ny = atlas.shape[:2]
    deep = rows + 2 * TSTEPS
    pixels = ny * LANES
    out = (per if joined else 1, width, pixels)
    count = peers if joined else peers * per
    return pl.pallas_call(
        functools.partial(transport_kernel, peers, per, joined, width, part),
        out_shape=[jax.ShapeDtypeStruct(out, BF16)] * count,
        in_specs=[spec(pltpu.SMEM)] * 2 + [spec(pltpu.VMEM)] * 6,
        out_specs=[spec(pltpu.VMEM)] * count,
        scratch_shapes=[
            pltpu.VMEM((2, deep, ny, width, LANES), F32),
            pltpu.VMEM((3, ny, deep, LANES), F32),
            pltpu.VMEM((7, ny, deep, LANES), F32),
        ],
        compiler_params=params(28),
        cost_estimate=cost(COST_T),
        name="transport",
    )(scalars, slots, atlas, vel, low, high, low0, high0)


def dot(a, b):
    return jnp.dot(a, b, preferred_element_type=F32)


def dot_full(a, b):
    return jnp.dot(a, b, preferred_element_type=F32, precision=lax.Precision.HIGHEST)


def halves(value):
    high = value.astype(BF16)
    return high, (value - high.astype(F32)).astype(BF16)


def fit_kernel(parts, peers, mask, density, *refs):
    blocks = refs[: parts * peers]
    outs = refs[parts * peers : parts * peers + peers]
    panel, gram, right, inverse, answer = refs[parts * peers + peers :]
    width, pixels = blocks[0].shape[1:]
    channels = panel.shape[0]
    share = channels // peers
    ny = pixels // LANES
    for k in range(peers):
        for part in range(parts):
            first = k * share + part * width
            panel[first : first + width, :] = blocks[k * parts + part][0]
    valid = mask[0] > 0
    every = panel[...]
    maps = density[0]
    masked = jnp.where(valid, every, jnp.zeros_like(every))
    contract = (((1,), (1,)), ((), ()))
    row = lax.broadcasted_iota(jnp.int32, (channels, channels), 0)
    column = lax.broadcasted_iota(jnp.int32, (channels, channels), 1)
    same = row == column
    gram[...] = lax.dot_general(every, masked, contract, preferred_element_type=F32) * (
        1.0 / pixels
    ) + jnp.where(same, RIDGE, 0.0)
    right[...] = lax.dot_general(maps, masked, contract, preferred_element_type=F32) * (
        1.0 / pixels
    )
    sums = jnp.sum(jnp.abs(gram[...]), axis=0, keepdims=True)
    bound_row = jnp.max(sums, axis=1, keepdims=True)
    bound = jnp.max(sums)
    start = 2.0 / (RIDGE + bound_row)
    spread = (bound_row - RIDGE) / (bound_row + RIDGE)

    def narrowed(spread):
        square = spread * spread
        return square / (2.0 - square), 2.0 / (2.0 - square)

    def doubled(scale):
        low = inverse[...].astype(BF16)
        left = jnp.where(same, 1.0, 0.0) - dot(gram[...].astype(BF16), low)
        inverse[...] = scale * (inverse[...] + dot(low, left.astype(BF16)))

    def refined():
        high, rest = halves(answer[...])
        gram_high, gram_rest = halves(gram[...])
        product = dot(high, gram_high) + (dot(rest, gram_high) + dot(high, gram_rest))
        left = (right[...] - product).astype(BF16)
        answer[...] = answer[...] + dot(left, inverse[...].astype(BF16))

    @pl.when(bound <= FAIR)
    def _():
        spread1, scale1 = narrowed(spread)
        spread2, scale2 = narrowed(spread1)
        _, scale3 = narrowed(spread2)
        inverse[...] = scale1 * (
            jnp.where(same, 2.0 * start, 0.0) - (start * start) * gram[...]
        )
        doubled(scale2)

        @pl.when(bound > EASY)
        def _():
            doubled(scale3)

        answer[...] = dot(right[...].astype(BF16), inverse[...].astype(BF16))
        refined()
        refined()

        @pl.when(bound > EASY)
        def _():
            refined()

    @pl.when(bound > FAIR)
    def _():
        inverse[...] = jnp.where(same, start, 0.0)

        def step(spread):
            left = jnp.where(same, 2.0, 0.0) - dot_full(gram[...], inverse[...])
            inverse[...] = dot_full(inverse[...], left)
            return spread * spread

        lax.while_loop(lambda spread: spread > 1e-4, step, jnp.max(spread))
        answer[...] = dot_full(right[...], inverse[...])
        for _ in range(3):
            left = right[...] - dot_full(answer[...], gram[...])
            answer[...] = answer[...] + dot_full(left, inverse[...])

    coefficient_t = answer[...].astype(BF16)
    coefficient = answer[...].T.astype(BF16)
    fitted = dot(coefficient_t, panel[...])
    residual = (fitted - maps.astype(F32)).astype(BF16)
    pushed = dot(coefficient, residual)
    gradient = jnp.where(valid, 2.0 * pushed, 0.0).astype(BF16)
    for k in range(peers):
        for y in range(ny):
            outs[k][y] = gradient[k * share : (k + 1) * share, y * LANES : (y + 1) * LANES]


def fit(mask, density, section, blocks, parts, peers):
    width, pixels = blocks[0].shape[1:]
    channels = width * parts * peers
    classes = density.shape[1]
    ny = pixels // LANES

    def one(block):
        at = section if block.shape[0] > 1 else 0
        return pl.BlockSpec((1, width, pixels), lambda i: (at, 0, 0))

    out = (ny, channels // peers, LANES)
    return pl.pallas_call(
        functools.partial(fit_kernel, parts, peers),
        grid=(1,),
        out_shape=[jax.ShapeDtypeStruct(out, BF16)] * peers,
        in_specs=[
            pl.BlockSpec((1, 1, pixels), lambda i: (section, 0, 0)),
            pl.BlockSpec((1, classes, pixels), lambda i: (section, 0, 0)),
        ]
        + [one(block) for block in blocks],
        out_specs=[pl.BlockSpec(out, lambda i: (0, 0, 0))] * peers,
        scratch_shapes=[
            pltpu.VMEM((channels, pixels), BF16),
            pltpu.VMEM((channels, channels), F32),
            pltpu.VMEM((classes, channels), F32),
            pltpu.VMEM((channels, channels), F32),
            pltpu.VMEM((classes, channels), F32),
        ],
        compiler_params=params(24),
        cost_estimate=cost(COST_F),
        name="fit",
    )(mask, density, *blocks)


def place_kernel(peers, per, section, scalars, slots, *refs):
    blocks = refs[:peers]
    out, sems = refs[-2], refs[-1]
    me = scalars[2]
    copies = [
        pltpu.make_async_copy(
            blocks[k], out.at[slots[(me ^ k) * per + section]], sems.at[k]
        )
        for k in range(peers)
    ]
    for copy in copies:
        copy.start()
    for copy in copies:
        copy.wait()


def place(scalars, slots, blocks, earlier, rows, section, per):
    peers = len(blocks)
    extra = [] if earlier is None else [earlier]
    return pl.pallas_call(
        functools.partial(place_kernel, peers, per, section),
        out_shape=jax.ShapeDtypeStruct((rows,) + blocks[0].shape, BF16),
        in_specs=[spec(pltpu.SMEM)] * 2
        + [spec(pltpu.VMEM)] * peers
        + [spec(pl.ANY)] * len(extra),
        out_specs=spec(pl.ANY),
        scratch_shapes=[pltpu.SemaphoreType.DMA((peers,))],
        input_output_aliases={2 + peers: 0} if extra else {},
        compiler_params=params(8),
        cost_estimate=cost(COST_P),
        name="place",
    )(scalars, slots, *blocks, *extra)


def body(atlas_features, velocity, section_density, pixel_mask, section_slice):
    rows, channels = atlas_features.shape[:2]
    slabs = lax.axis_size("gz")
    slab = lax.axis_index("gz")
    peers = lax.axis_size(("gy", "af"))
    me = lax.axis_index(("gy", "af"))
    per = section_density.shape[0]
    chunks = max(1, channels // CHUNK)
    width = channels // chunks

    atlas = jnp.transpose(atlas_features, (0, 2, 1, 3))
    vel = jnp.transpose(velocity, (0, 2, 1, 3))
    mask = pixel_mask.reshape(per, 1, -1)
    slots = section_slice - slab * rows
    scalars = jnp.stack([slab > 0, slab < slabs - 1, me]).astype(jnp.int32)

    edges = pack(atlas, vel, width, chunks)
    upward = [(i, i + 1) for i in range(slabs - 1)]
    downward = [(i + 1, i) for i in range(slabs - 1)]
    halos = []
    for part in range(chunks):
        low = lax.ppermute(edges[2 * part + 1], "gz", upward)
        high = lax.ppermute(edges[2 * part], "gz", downward)
        halos.append((low, high))

    def swap(block, k):
        if k == 0:
            return block
        return lax.ppermute(block, ("gy", "af"), [(i, i ^ k) for i in range(peers)])

    arrived = {}
    for part in range(chunks):
        joined = part < chunks - 1
        order = slots
        if part > 0:
            order, _ = lax.optimization_barrier((slots, moved[0]))
        moved = transport(
            scalars, order, atlas, vel, *halos[part], *halos[0], width, part, peers, per, joined
        )
        if part > 0:
            moved, _ = lax.optimization_barrier((moved, arrived[0, peers // 2, part - 1]))
        for s in range(1 if joined else per):
            for k in range(peers):
                block = swap(moved[k if joined else k * per + s], k)
                for section in range(per) if joined else [s]:
                    arrived[section, k, part] = block

    result = None
    for s in range(per):
        blocks = [arrived[s, k, part] for k in range(peers) for part in range(chunks)]
        gradients = fit(mask, section_density, s, blocks, chunks, peers)
        returned = [swap(gradients[k], k) for k in range(peers)]
        result = place(scalars, slots, returned, result, rows, s, per)
    return jnp.transpose(result, (0, 2, 1, 3))


def solution(mesh):
    return jax.shard_map(
        body,
        mesh=mesh,
        in_specs=(
            P(("groups", "gz"), ("gy", "af"), None, None),
            P(None, ("groups", "gz"), None, None),
            P(("groups", "gz", "gy", "af"), None, None),
            P(("groups", "gz", "gy", "af"), None),
            P(("groups", "gz")),
        ),
        out_specs=P(("groups", "gz"), ("gy", "af"), None, None),
        check_vma=False,
    )
```

```python
import functools
import itertools

import jax
import jax.numpy as jnp
from jax import lax
from jax.experimental import pallas as pl
from jax.experimental.pallas import tpu as pltpu
from jax.sharding import PartitionSpec as P

TSTEPS = 4
RATE = 0.04
RIDGE = 0.25
LANES = 128
F32 = jnp.float32
BF16 = jnp.bfloat16
VEL_ROWS = 16
WIDTHS = (32, 32)
COST_I, COST_T, COST_F, COST_P = 4 * 10**9, 6 * 10**9, 3 * 10**9, 15 * 10**8
EASY = 1.08
FAIR = 3.8


def spec(memory_space):
    return pl.BlockSpec(memory_space=memory_space)


def cost(count):
    return pl.CostEstimate(flops=count, bytes_accessed=0, transcendentals=0)


def params(mib):
    return pltpu.CompilerParams(vmem_limit_bytes=mib << 20)


def odd_slab():
    return lax.rem(lax.axis_index("gz"), 2)


def pack_kernel(widths, atlas, vel, *refs):
    outs, (held, boxes, sems) = refs[:-3], refs[-3:]
    rows, ny = atlas.shape[:2]
    odd = odd_slab()
    slots = TSTEPS - 1
    copies = []
    count = itertools.count()

    def move(source, target):
        copies.append(pltpu.make_async_copy(source, target, sems.at[next(count)]))
        copies[-1].start()

    move(vel, held)
    start = 0
    for part, width in enumerate(widths):
        for side in range(2):
            first = jnp.where(odd == side, rows - TSTEPS, 0)
            for step in range(TSTEPS):
                move(
                    atlas.at[first + step, :, pl.ds(start, width), :],
                    outs[2 * part + side].at[:, pl.ds(step * width, width), :],
                )
        start += width
    copies.pop(0).wait()
    speed = held[...].astype(F32)
    filler = jnp.zeros((ny, VEL_ROWS - 3 * slots, LANES), F32)
    edges = []
    for first in (0, rows - slots):
        lines = [speed[k, :, first : first + slots, :] for k in range(3)]
        edges.append(jnp.concatenate(lines + [filler], axis=1))
    for side in range(2):
        boxes[side] = jnp.where(odd == side, edges[1], edges[0]).astype(BF16)
        move(boxes.at[side], outs[side].at[:, pl.ds(TSTEPS * widths[0], VEL_ROWS), :])
    for copy in copies:
        copy.wait()


def pack(atlas, vel, widths):
    ny = atlas.shape[1]
    shapes = []
    for part, width in enumerate(widths):
        rows = TSTEPS * width + (VEL_ROWS if part == 0 else 0)
        shapes += [jax.ShapeDtypeStruct((ny, rows, LANES), BF16)] * 2
    return pl.pallas_call(
        functools.partial(pack_kernel, widths),
        out_shape=shapes,
        in_specs=[spec(pl.ANY)] * 2,
        out_specs=[spec(pl.ANY)] * len(shapes),
        scratch_shapes=[
            pltpu.VMEM(vel.shape, BF16),
            pltpu.VMEM((2, ny, VEL_ROWS, LANES), BF16),
            pltpu.SemaphoreType.DMA((2 * len(widths) * TSTEPS + 3,)),
        ],
        compiler_params=params(8),
        name="pack_edges",
    )(*(pltpu.with_memory_space_constraint(x, pltpu.HBM) for x in (atlas, vel)))


def set_weights(speed, coef, inside):
    lane = lax.broadcasted_iota(jnp.int32, (1,) + speed.shape[2:], 2)
    for y in range(speed.shape[1]):
        total = jnp.zeros(lane.shape, F32)
        for k in range(3):
            v = speed[k, y : y + 1]
            from_low = jnp.maximum(v, 0.0) + RATE
            from_high = RATE - jnp.minimum(v, 0.0)
            total = total + (from_low + from_high)
            if k == 2:
                from_low = jnp.where(lane == 0, 0.0, from_low)
                from_high = jnp.where(lane == LANES - 1, 0.0, from_high)
            coef[2 * k + 1, y : y + 1] = jnp.where(inside, from_low, 0.0)
            coef[2 * k + 2, y : y + 1] = jnp.where(inside, from_high, 0.0)
        coef[0, y : y + 1] = jnp.where(inside, 1.0 - total, 0.0)


def advance(coef, source, target, z, shift=0):
    at = z - shift
    ny = source.shape[1]
    for y in range(ny):
        weight = [coef[i, y, pl.ds(z, 1), :] for i in range(7)]
        center = source[at, y]
        total = weight[0] * center
        total = total + weight[1] * source[at - 1, y]
        total = total + weight[2] * source[at + 1, y]
        if y > 0:
            total = total + weight[3] * source[at, y - 1]
        if y < ny - 1:
            total = total + weight[4] * source[at, y + 1]
        total = total + weight[5] * pltpu.roll(center, 1, axis=1)
        total = total + weight[6] * pltpu.roll(center, LANES - 1, axis=1)
        target[z, y] = total


def advance_pairs(coef, source, target, pairs, first, shift=0):
    def step(i, carry):
        z = first(i)
        advance(coef, source, target, z, shift)
        advance(coef, source, target, z + 1, shift)
        return carry

    lax.fori_loop(0, pairs, step, 0)


def inner_kernel(atlas, vel, one, two, three, state, speed, coef):
    rows = atlas.shape[0]
    speed[...] = vel[...].astype(F32)
    set_weights(speed, coef, True)

    def load(z, carry):
        state[z] = atlas[z].astype(F32)
        return carry

    lax.fori_loop(0, rows, load, 0)
    levels = (state, one, two, three)
    for step in range(TSTEPS - 1):
        pairs = (rows - 2 * (step + 1)) // 2
        first = step + 1
        advance_pairs(coef, levels[step], levels[step + 1], pairs, lambda i: first + 2 * i)


def inner(atlas, vel):
    level = jax.ShapeDtypeStruct(atlas.shape, F32)
    return pl.pallas_call(
        inner_kernel,
        out_shape=[level] * (TSTEPS - 1),
        in_specs=[spec(pltpu.VMEM)] * 2,
        out_specs=[spec(pltpu.VMEM)] * (TSTEPS - 1),
        scratch_shapes=[
            pltpu.VMEM(atlas.shape, F32),
            pltpu.VMEM(vel.shape, F32),
            pltpu.VMEM((7,) + vel.shape[1:], F32),
        ],
        compiler_params=params(24),
        cost_estimate=cost(COST_I),
        name="inner_steps",
    )(atlas, vel)


def transport_kernel(
    peers, per, joined, width, start, slots, atlas, vel, one, two, one0, two0, *refs
):
    inner_levels, refs = refs[: TSTEPS - 1], refs[TSTEPS - 1 :]
    outs, (state, speed, coef) = refs[:-3], refs[-3:]
    rows, ny = atlas.shape[:2]
    tail = slice(one0.shape[1] - VEL_ROWS, one0.shape[1])
    deep = rows + 2 * TSTEPS
    edge = TSTEPS - 1
    slab, slabs = lax.axis_index("gz"), lax.axis_size("gz")
    me = lax.axis_index(("gy", "af"))
    odd = odd_slab() > 0
    has_low, has_high = slab > 0, slab < slabs - 1

    def sides(one, two):
        one, two = one.astype(F32), two.astype(F32)
        return jnp.where(odd, one, two), jnp.where(odd, two, one)

    below, above = sides(one0[:, tail, :], two0[:, tail, :])
    for k in range(3):
        speed[k, :, TSTEPS : TSTEPS + rows, :] = vel[k].astype(F32)
        speed[k, :, 1:TSTEPS, :] = below[:, edge * k : edge * (k + 1), :]
        speed[k, :, TSTEPS + rows : TSTEPS + rows + edge, :] = above[:, edge * k : edge * (k + 1), :]
    place = lax.broadcasted_iota(jnp.int32, (1, deep, LANES), 1)
    inside = ((place >= TSTEPS) | has_low) & ((place < TSTEPS + rows) | has_high)
    set_weights(speed, coef, inside & (place > 0) & (place < deep - 1))

    channels = slice(start, start + width)
    for z in (0, 1, rows - 2, rows - 1):
        state[0, z + TSTEPS] = atlas[z, :, channels, :].astype(F32)
    for step in range(TSTEPS):
        span = slice(step * width, (step + 1) * width)
        low, high = sides(one[:, span, :], two[:, span, :])
        state[0, step] = low
        state[0, step + TSTEPS + rows] = high
    for level in range(1, TSTEPS):
        for z in sorted({level, level + 1, rows - 2 - level, rows - 1 - level}):
            state[level, z + TSTEPS] = inner_levels[level - 1][z, :, channels, :]
    for step in range(TSTEPS):

        def first(i):
            return jnp.where(i < 2, step + 1 + 2 * i, deep - 9 - step + 2 * i)

        target = state.at[(step + 1) % TSTEPS]
        advance_pairs(coef, state.at[step], target, TSTEPS, first)
    if rows > 2 * TSTEPS:
        source = inner_levels[-1].at[:, :, channels, :]
        pairs = (rows - 2 * TSTEPS) // 2
        advance_pairs(coef, source, state.at[0], pairs, lambda i: 2 * TSTEPS + 2 * i, TSTEPS)

    for k in range(peers):
        for s in range(per):
            z = slots[(me ^ k) * per + s] - slab * rows + TSTEPS
            out = outs[k].at[s] if joined else outs[k * per + s].at[0]
            for y in range(ny):
                value = state[0, z, y].astype(BF16)
                out[:, y * LANES : (y + 1) * LANES] = value


def transport(slots, atlas, vel, one, two, one0, two0, levels, width, start, peers, per, joined):
    rows, ny = atlas.shape[:2]
    deep = rows + 2 * TSTEPS
    pixels = ny * LANES
    out = (per if joined else 1, width, pixels)
    count = peers if joined else peers * per
    return pl.pallas_call(
        functools.partial(transport_kernel, peers, per, joined, width, start),
        out_shape=[jax.ShapeDtypeStruct(out, BF16)] * count,
        in_specs=[spec(pltpu.SMEM)] + [spec(pltpu.VMEM)] * (6 + len(levels)),
        out_specs=[spec(pltpu.VMEM)] * count,
        scratch_shapes=[
            pltpu.VMEM((TSTEPS, deep, ny, width, LANES), F32),
            pltpu.VMEM((3, ny, deep, LANES), F32),
            pltpu.VMEM((7, ny, deep, LANES), F32),
        ],
        compiler_params=params(28),
        cost_estimate=cost(COST_T),
        name="transport",
    )(slots, atlas, vel, one, two, one0, two0, *levels)


def dot(a, b):
    return jnp.dot(a, b, preferred_element_type=F32)


def dot_full(a, b):
    return jnp.dot(a, b, preferred_element_type=F32, precision=lax.Precision.HIGHEST)


def halves(value):
    high = value.astype(BF16)
    return high, (value - high.astype(F32)).astype(BF16)


def fit_kernel(parts, peers, mask, density, *refs):
    blocks = refs[: parts * peers]
    outs = refs[parts * peers : parts * peers + peers]
    panel, gram, right, inverse, answer = refs[parts * peers + peers :]
    pixels = panel.shape[1]
    channels = panel.shape[0]
    share = channels // peers
    ny = pixels // LANES
    for k in range(peers):
        first = k * share
        for block in blocks[k * parts : (k + 1) * parts]:
            panel[first : first + block.shape[1], :] = block[0]
            first += block.shape[1]
    valid = mask[0] > 0
    every = panel[...]
    maps = density[0]
    masked = jnp.where(valid, every, jnp.zeros_like(every))
    contract = (((1,), (1,)), ((), ()))
    row = lax.broadcasted_iota(jnp.int32, (channels, channels), 0)
    column = lax.broadcasted_iota(jnp.int32, (channels, channels), 1)
    same = row == column
    gram[...] = lax.dot_general(every, masked, contract, preferred_element_type=F32) * (
        1.0 / pixels
    ) + jnp.where(same, RIDGE, 0.0)
    right[...] = lax.dot_general(maps, masked, contract, preferred_element_type=F32) * (
        1.0 / pixels
    )
    sums = jnp.sum(jnp.abs(gram[...]), axis=0, keepdims=True)
    bound_row = jnp.max(sums, axis=1, keepdims=True)
    bound = jnp.max(sums)
    start = 2.0 / (RIDGE + bound_row)
    spread = (bound_row - RIDGE) / (bound_row + RIDGE)

    def narrowed(spread):
        square = spread * spread
        return square / (2.0 - square), 2.0 / (2.0 - square)

    def doubled(scale):
        low = inverse[...].astype(BF16)
        left = jnp.where(same, 1.0, 0.0) - dot(gram[...].astype(BF16), low)
        inverse[...] = scale * (inverse[...] + dot(low, left.astype(BF16)))

    def refined():
        high, rest = halves(answer[...])
        gram_high, gram_rest = halves(gram[...])
        product = dot(high, gram_high) + (dot(rest, gram_high) + dot(high, gram_rest))
        left = (right[...] - product).astype(BF16)
        answer[...] = answer[...] + dot(left, inverse[...].astype(BF16))

    @pl.when(bound <= FAIR)
    def _():
        spread1, scale1 = narrowed(spread)
        spread2, scale2 = narrowed(spread1)
        _, scale3 = narrowed(spread2)
        inverse[...] = scale1 * (
            jnp.where(same, 2.0 * start, 0.0) - (start * start) * gram[...]
        )
        doubled(scale2)

        @pl.when(bound > EASY)
        def _():
            doubled(scale3)

        answer[...] = dot(right[...].astype(BF16), inverse[...].astype(BF16))
        refined()
        refined()

        @pl.when(bound > EASY)
        def _():
            refined()

    @pl.when(bound > FAIR)
    def _():
        inverse[...] = jnp.where(same, start, 0.0)

        def step(spread):
            left = jnp.where(same, 2.0, 0.0) - dot_full(gram[...], inverse[...])
            inverse[...] = dot_full(inverse[...], left)
            return spread * spread

        lax.while_loop(lambda spread: spread > 1e-4, step, jnp.max(spread))
        answer[...] = dot_full(right[...], inverse[...])
        for _ in range(3):
            left = right[...] - dot_full(answer[...], gram[...])
            answer[...] = answer[...] + dot_full(left, inverse[...])

    coefficient_t = answer[...].astype(BF16)
    coefficient = answer[...].T.astype(BF16)
    fitted = dot(coefficient_t, panel[...])
    residual = (fitted - maps.astype(F32)).astype(BF16)
    pushed = dot(coefficient, residual)
    gradient = jnp.where(valid, 2.0 * pushed, 0.0).astype(BF16)
    for k in range(peers):
        for y in range(ny):
            outs[k][y] = gradient[k * share : (k + 1) * share, y * LANES : (y + 1) * LANES]


def fit(mask, density, section, blocks, parts, peers):
    pixels = blocks[0].shape[2]
    channels = sum(block.shape[1] for block in blocks)
    classes = density.shape[1]
    ny = pixels // LANES

    def one(block):
        at = section if block.shape[0] > 1 else 0
        return pl.BlockSpec((1,) + block.shape[1:], lambda i: (at, 0, 0))

    out = (ny, channels // peers, LANES)
    return pl.pallas_call(
        functools.partial(fit_kernel, parts, peers),
        grid=(1,),
        out_shape=[jax.ShapeDtypeStruct(out, BF16)] * peers,
        in_specs=[
            pl.BlockSpec((1, 1, pixels), lambda i: (section, 0, 0)),
            pl.BlockSpec((1, classes, pixels), lambda i: (section, 0, 0)),
        ]
        + [one(block) for block in blocks],
        out_specs=[pl.BlockSpec(out, lambda i: (0, 0, 0))] * peers,
        scratch_shapes=[
            pltpu.VMEM((channels, pixels), BF16),
            pltpu.VMEM((channels, channels), F32),
            pltpu.VMEM((classes, channels), F32),
            pltpu.VMEM((channels, channels), F32),
            pltpu.VMEM((classes, channels), F32),
        ],
        compiler_params=params(24),
        cost_estimate=cost(COST_F),
        name="fit",
    )(mask, density, *blocks)


def place_kernel(peers, per, section, slots, *refs):
    blocks = refs[:peers]
    out, sems = refs[-2], refs[-1]
    me = lax.axis_index(("gy", "af"))
    first = lax.axis_index("gz") * out.shape[0]
    copies = [
        pltpu.make_async_copy(
            blocks[k], out.at[slots[(me ^ k) * per + section] - first], sems.at[k]
        )
        for k in range(peers)
    ]
    for copy in copies:
        copy.start()
    for copy in copies:
        copy.wait()


def place(slots, blocks, earlier, rows, section, per):
    peers = len(blocks)
    extra = [] if earlier is None else [earlier]
    return pl.pallas_call(
        functools.partial(place_kernel, peers, per, section),
        out_shape=jax.ShapeDtypeStruct((rows,) + blocks[0].shape, BF16),
        in_specs=[spec(pltpu.SMEM)]
        + [spec(pltpu.VMEM)] * peers
        + [spec(pl.ANY)] * len(extra),
        out_specs=spec(pl.ANY),
        scratch_shapes=[pltpu.SemaphoreType.DMA((peers,))],
        input_output_aliases={1 + peers: 0} if extra else {},
        compiler_params=params(8),
        cost_estimate=cost(COST_P),
        name="place",
    )(slots, *blocks, *extra)


def body(atlas_features, velocity, section_density, pixel_mask, section_slice):
    rows, channels = atlas_features.shape[:2]
    slabs = lax.axis_size("gz")
    peers = lax.axis_size(("gy", "af"))
    per = section_density.shape[0]
    widths = WIDTHS if sum(WIDTHS) == channels else (channels,)
    chunks = len(widths)

    atlas = jnp.transpose(atlas_features, (0, 2, 1, 3))
    vel = jnp.transpose(velocity, (0, 2, 1, 3))
    mask = pixel_mask.reshape(per, 1, -1)
    slots = section_slice

    edges = pack(atlas, vel, widths)
    ones = [(i, i ^ 1) for i in range(slabs)]
    twos = [(i, i + 1) for i in range(1, slabs - 1, 2)]
    twos += [(j, i) for i, j in twos]
    halos = []
    for part in range(chunks):
        one = lax.ppermute(edges[2 * part], "gz", ones)
        two = lax.ppermute(edges[2 * part + 1], "gz", twos)
        halos.append((one, two))

    own, _ = lax.optimization_barrier((atlas, edges[0]))
    levels = inner(own, vel)

    def swap(block, k):
        if k == 0:
            return block
        return lax.ppermute(block, ("gy", "af"), [(i, i ^ k) for i in range(peers)])

    arrived = {}
    start = 0
    for part, width in enumerate(widths):
        joined = part < chunks - 1
        order = slots
        if part > 0:
            order, _ = lax.optimization_barrier((slots, moved[0]))
        moved = transport(
            order, atlas, vel, *halos[part], *halos[0], levels, width, start, peers, per, joined
        )
        start += width
        if part > 0:
            moved, _ = lax.optimization_barrier((moved, arrived[0, peers // 2, part - 1]))
        for s in range(1 if joined else per):
            for k in range(peers):
                block = swap(moved[k if joined else k * per + s], k)
                for section in range(per) if joined else [s]:
                    arrived[section, k, part] = block

    result = None
    for s in range(per):
        blocks = [arrived[s, k, part] for k in range(peers) for part in range(chunks)]
        gradients = fit(mask, section_density, s, blocks, chunks, peers)
        returned = [swap(gradients[k], k) for k in range(peers)]
        result = place(slots, returned, result, rows, s, per)
    return jnp.transpose(result, (0, 2, 1, 3))


def solution(mesh):
    return jax.shard_map(
        body,
        mesh=mesh,
        in_specs=(
            P(("groups", "gz"), ("gy", "af"), None, None),
            P(None, ("groups", "gz"), None, None),
            P(("groups", "gz", "gy", "af"), None, None),
            P(("groups", "gz", "gy", "af"), None),
            P(("groups", "gz")),
        ),
        out_specs=P(("groups", "gz"), ("gy", "af"), None, None),
        check_vma=False,
    )
```

```python
import functools
import itertools

import jax
import jax.numpy as jnp
from jax import lax
from jax.experimental import pallas as pl
from jax.experimental.pallas import tpu as pltpu
from jax.sharding import PartitionSpec as P

TSTEPS = 4
RATE = 0.04
RIDGE = 0.25
LANES = 128
F32 = jnp.float32
BF16 = jnp.bfloat16
VEL_ROWS = 16
WIDTHS = (32, 32)
COST_I, COST_T, COST_F, COST_P = 4 * 10**9, 10**9, 3 * 10**9, 15 * 10**8
EASY = 1.08
FAIR = 3.8


def spec(memory_space):
    return pl.BlockSpec(memory_space=memory_space)


def cost(count):
    return pl.CostEstimate(flops=count, bytes_accessed=0, transcendentals=0)


def params(mib):
    return pltpu.CompilerParams(vmem_limit_bytes=mib << 20)


def odd_slab():
    return lax.rem(lax.axis_index("gz"), 2)


def pack_kernel(width, start, atlas, vel, low, high, held, boxes, sems):
    outs = (low, high)
    rows, ny = atlas.shape[:2]
    odd = odd_slab()
    slots = TSTEPS - 1
    copies = []
    count = itertools.count()

    def move(source, target):
        copies.append(pltpu.make_async_copy(source, target, sems.at[next(count)]))
        copies[-1].start()

    if start == 0:
        move(vel, held)
    for side in range(2):
        first = jnp.where(odd == side, rows - TSTEPS, 0)
        for step in range(TSTEPS):
            move(
                atlas.at[first + step, :, pl.ds(start, width), :],
                outs[side].at[:, pl.ds(step * width, width), :],
            )
    if start == 0:
        copies.pop(0).wait()
        speed = held[...].astype(F32)
        filler = jnp.zeros((ny, VEL_ROWS - 3 * slots, LANES), F32)
        edges = []
        for first in (0, rows - slots):
            lines = [speed[k, :, first : first + slots, :] for k in range(3)]
            edges.append(jnp.concatenate(lines + [filler], axis=1))
        for side in range(2):
            boxes[side] = jnp.where(odd == side, edges[1], edges[0]).astype(BF16)
            move(boxes.at[side], outs[side].at[:, pl.ds(TSTEPS * width, VEL_ROWS), :])
    for copy in copies:
        copy.wait()


def pack(atlas, vel, width, start):
    ny = atlas.shape[1]
    rows = TSTEPS * width + (VEL_ROWS if start == 0 else 0)
    return pl.pallas_call(
        functools.partial(pack_kernel, width, start),
        out_shape=[jax.ShapeDtypeStruct((ny, rows, LANES), BF16)] * 2,
        in_specs=[spec(pl.ANY)] * 2,
        out_specs=[spec(pl.ANY)] * 2,
        scratch_shapes=[
            pltpu.VMEM(vel.shape, BF16),
            pltpu.VMEM((2, ny, VEL_ROWS, LANES), BF16),
            pltpu.SemaphoreType.DMA((2 * TSTEPS + 3,)),
        ],
        compiler_params=params(8),
        name="pack_edges",
    )(*(pltpu.with_memory_space_constraint(x, pltpu.HBM) for x in (atlas, vel)))


def set_weights(speed, coef, inside):
    lane = lax.broadcasted_iota(jnp.int32, (1,) + speed.shape[2:], 2)
    for y in range(speed.shape[1]):
        total = jnp.zeros(lane.shape, F32)
        for k in range(3):
            v = speed[k, y : y + 1]
            from_low = jnp.maximum(v, 0.0) + RATE
            from_high = RATE - jnp.minimum(v, 0.0)
            total = total + (from_low + from_high)
            if k == 2:
                from_low = jnp.where(lane == 0, 0.0, from_low)
                from_high = jnp.where(lane == LANES - 1, 0.0, from_high)
            coef[2 * k + 1, y : y + 1] = jnp.where(inside, from_low, 0.0)
            coef[2 * k + 2, y : y + 1] = jnp.where(inside, from_high, 0.0)
        coef[0, y : y + 1] = jnp.where(inside, 1.0 - total, 0.0)


def advance(coef, source, target, z, shift=0):
    at = z - shift
    ny = source.shape[1]
    for y in range(ny):
        weight = [coef[i, y, pl.ds(z, 1), :] for i in range(7)]
        center = source[at, y]
        total = weight[0] * center
        total = total + weight[1] * source[at - 1, y]
        total = total + weight[2] * source[at + 1, y]
        if y > 0:
            total = total + weight[3] * source[at, y - 1]
        if y < ny - 1:
            total = total + weight[4] * source[at, y + 1]
        total = total + weight[5] * pltpu.roll(center, 1, axis=1)
        total = total + weight[6] * pltpu.roll(center, LANES - 1, axis=1)
        target[z, y] = total


def advance_pairs(coef, source, target, pairs, first, shift=0):
    def step(i, carry):
        z = first(i)
        advance(coef, source, target, z, shift)
        advance(coef, source, target, z + 1, shift)
        return carry

    lax.fori_loop(0, pairs, step, 0)


def inner_kernel(atlas, vel, one, two, three, state, speed, coef):
    rows = atlas.shape[0]
    speed[...] = vel[...].astype(F32)
    set_weights(speed, coef, True)

    def load(z, carry):
        state[z] = atlas[z].astype(F32)
        return carry

    lax.fori_loop(0, rows, load, 0)
    levels = (state, one, two, three)
    for step in range(TSTEPS - 1):
        pairs = (rows - 2 * (step + 1)) // 2
        first = step + 1
        advance_pairs(coef, levels[step], levels[step + 1], pairs, lambda i: first + 2 * i)


def inner(atlas, vel):
    level = jax.ShapeDtypeStruct(atlas.shape, F32)
    return pl.pallas_call(
        inner_kernel,
        out_shape=[level] * (TSTEPS - 1),
        in_specs=[spec(pltpu.VMEM)] * 2,
        out_specs=[spec(pltpu.VMEM)] * (TSTEPS - 1),
        scratch_shapes=[
            pltpu.VMEM(atlas.shape, F32),
            pltpu.VMEM(vel.shape, F32),
            pltpu.VMEM((7,) + vel.shape[1:], F32),
        ],
        compiler_params=params(24),
        cost_estimate=cost(COST_I),
        name="inner_steps",
    )(atlas, vel)


def side_steps(high, width, start, atlas, vel, halo, halo0, levels, state, speed, coef):
    rows, ny = atlas.shape[:2]
    deep = rows + 2 * TSTEPS
    edge = TSTEPS - 1
    slab, slabs = lax.axis_index("gz"), lax.axis_size("gz")
    has = jnp.where(high, slab < slabs - 1, slab > 0)
    beyond = halo0[:, halo0.shape[1] - VEL_ROWS :, :].astype(F32)
    for k in range(3):
        lines = beyond[:, edge * k : edge * (k + 1), :]
        speed[k, :, TSTEPS : TSTEPS + rows, :] = vel[k].astype(F32)
        speed[k, :, 1:TSTEPS, :] = lines
        speed[k, :, TSTEPS + rows : TSTEPS + rows + edge, :] = lines
    place = lax.broadcasted_iota(jnp.int32, (1, deep, LANES), 1)
    inside = ((place >= TSTEPS) & (place < TSTEPS + rows)) | has
    set_weights(speed, coef, inside & (place > 0) & (place < deep - 1))

    channels = slice(start, start + width)
    base = jnp.where(high, TSTEPS + rows, 0)
    for step in range(TSTEPS):
        state[0, base + step] = halo[:, step * width : (step + 1) * width, :].astype(F32)
    for i in range(2):
        z = jnp.where(high, rows - 2, 0) + i
        state[0, z + TSTEPS] = atlas[z, :, channels, :].astype(F32)
        for level in range(1, TSTEPS):
            z = jnp.where(high, rows - 2 - level, level) + i
            state[level, z + TSTEPS] = levels[level - 1][z, :, channels, :]
    for step in range(TSTEPS):
        first = jnp.where(high, deep - 5 - step, step + 1)
        target = state.at[(step + 1) % TSTEPS]
        advance_pairs(coef, state.at[step], target, TSTEPS // 2, lambda i: first + 2 * i)


def first_kernel(width, start, atlas, vel, halo, halo0, *refs):
    levels, (done, state, speed, coef) = refs[: TSTEPS - 1], refs[TSTEPS - 1 :]
    high = odd_slab() == 0
    side_steps(high, width, start, atlas, vel, halo, halo0, levels, state, speed, coef)
    first = jnp.where(high, atlas.shape[0] - TSTEPS, 0)
    for i in range(TSTEPS):
        done[i] = state[0, first + TSTEPS + i].astype(BF16)


def second_kernel(peers, per, joined, width, start, slots, atlas, vel, halo, halo0, *refs):
    levels, done, refs = refs[: TSTEPS - 1], refs[TSTEPS - 1], refs[TSTEPS:]
    outs, (moved, state, speed, coef) = refs[:-4], refs[-4:]
    rows, ny = atlas.shape[:2]
    high = odd_slab() > 0
    side_steps(high, width, start, atlas, vel, halo, halo0, levels, state, speed, coef)
    if rows > 2 * TSTEPS:
        source = levels[-1].at[:, :, start : start + width, :]
        pairs = (rows - 2 * TSTEPS) // 2
        advance_pairs(coef, source, state.at[0], pairs, lambda i: 2 * TSTEPS + 2 * i, TSTEPS)
        for z in range(TSTEPS, rows - TSTEPS):
            moved[z] = state[0, z + TSTEPS].astype(BF16)
    first = jnp.where(high, rows - TSTEPS, 0)
    other = rows - TSTEPS - first
    for i in range(TSTEPS):
        moved[first + i] = state[0, first + TSTEPS + i].astype(BF16)
        moved[other + i] = done[i]
    me = lax.axis_index(("gy", "af"))
    slab = lax.axis_index("gz")
    for k in range(peers):
        for s in range(per):
            z = slots[(me ^ k) * per + s] - slab * rows
            out = outs[k].at[s] if joined else outs[k * per + s].at[0]
            for y in range(ny):
                out[:, y * LANES : (y + 1) * LANES] = moved[z, y]


def side_scratch(atlas, width):
    rows, ny = atlas.shape[:2]
    deep = rows + 2 * TSTEPS
    return [
        pltpu.VMEM((TSTEPS, deep, ny, width, LANES), F32),
        pltpu.VMEM((3, ny, deep, LANES), F32),
        pltpu.VMEM((7, ny, deep, LANES), F32),
    ]


def first_side(atlas, vel, halo, halo0, levels, width, start):
    return pl.pallas_call(
        functools.partial(first_kernel, width, start),
        out_shape=jax.ShapeDtypeStruct((TSTEPS, atlas.shape[1], width, LANES), BF16),
        in_specs=[spec(pltpu.VMEM)] * (4 + len(levels)),
        out_specs=spec(pltpu.VMEM),
        scratch_shapes=side_scratch(atlas, width),
        compiler_params=params(28),
        cost_estimate=cost(COST_T),
        name="first_side",
    )(atlas, vel, halo, halo0, *levels)


def second_side(slots, atlas, vel, halo, halo0, levels, done, width, start, peers, per, joined):
    rows, ny = atlas.shape[:2]
    out = (per if joined else 1, width, ny * LANES)
    count = peers if joined else peers * per
    return pl.pallas_call(
        functools.partial(second_kernel, peers, per, joined, width, start),
        out_shape=[jax.ShapeDtypeStruct(out, BF16)] * count,
        in_specs=[spec(pltpu.SMEM)] + [spec(pltpu.VMEM)] * (5 + len(levels)),
        out_specs=[spec(pltpu.VMEM)] * count,
        scratch_shapes=[pltpu.VMEM((rows, ny, width, LANES), BF16)] + side_scratch(atlas, width),
        compiler_params=params(28),
        cost_estimate=cost(COST_T),
        name="second_side",
    )(slots, atlas, vel, halo, halo0, *levels, done)


def dot(a, b):
    return jnp.dot(a, b, preferred_element_type=F32)


def dot_full(a, b):
    return jnp.dot(a, b, preferred_element_type=F32, precision=lax.Precision.HIGHEST)


def halves(value):
    high = value.astype(BF16)
    return high, (value - high.astype(F32)).astype(BF16)


def fit_kernel(parts, peers, mask, density, *refs):
    blocks = refs[: parts * peers]
    outs = refs[parts * peers : parts * peers + peers]
    panel, gram, right, inverse, answer = refs[parts * peers + peers :]
    pixels = panel.shape[1]
    channels = panel.shape[0]
    share = channels // peers
    ny = pixels // LANES
    for k in range(peers):
        first = k * share
        for block in blocks[k * parts : (k + 1) * parts]:
            panel[first : first + block.shape[1], :] = block[0]
            first += block.shape[1]
    valid = mask[0] > 0
    every = panel[...]
    maps = density[0]
    masked = jnp.where(valid, every, jnp.zeros_like(every))
    contract = (((1,), (1,)), ((), ()))
    row = lax.broadcasted_iota(jnp.int32, (channels, channels), 0)
    column = lax.broadcasted_iota(jnp.int32, (channels, channels), 1)
    same = row == column
    gram[...] = lax.dot_general(every, masked, contract, preferred_element_type=F32) * (
        1.0 / pixels
    ) + jnp.where(same, RIDGE, 0.0)
    right[...] = lax.dot_general(maps, masked, contract, preferred_element_type=F32) * (
        1.0 / pixels
    )
    sums = jnp.sum(jnp.abs(gram[...]), axis=0, keepdims=True)
    bound_row = jnp.max(sums, axis=1, keepdims=True)
    bound = jnp.max(sums)
    start = 2.0 / (RIDGE + bound_row)
    spread = (bound_row - RIDGE) / (bound_row + RIDGE)

    def narrowed(spread):
        square = spread * spread
        return square / (2.0 - square), 2.0 / (2.0 - square)

    def doubled(scale):
        low = inverse[...].astype(BF16)
        left = jnp.where(same, 1.0, 0.0) - dot(gram[...].astype(BF16), low)
        inverse[...] = scale * (inverse[...] + dot(low, left.astype(BF16)))

    def refined():
        high, rest = halves(answer[...])
        gram_high, gram_rest = halves(gram[...])
        product = dot(high, gram_high) + (dot(rest, gram_high) + dot(high, gram_rest))
        left = (right[...] - product).astype(BF16)
        answer[...] = answer[...] + dot(left, inverse[...].astype(BF16))

    @pl.when(bound <= FAIR)
    def _():
        spread1, scale1 = narrowed(spread)
        spread2, scale2 = narrowed(spread1)
        _, scale3 = narrowed(spread2)
        inverse[...] = scale1 * (
            jnp.where(same, 2.0 * start, 0.0) - (start * start) * gram[...]
        )
        doubled(scale2)

        @pl.when(bound > EASY)
        def _():
            doubled(scale3)

        answer[...] = dot(right[...].astype(BF16), inverse[...].astype(BF16))
        refined()
        refined()

        @pl.when(bound > EASY)
        def _():
            refined()

    @pl.when(bound > FAIR)
    def _():
        inverse[...] = jnp.where(same, start, 0.0)

        def step(spread):
            left = jnp.where(same, 2.0, 0.0) - dot_full(gram[...], inverse[...])
            inverse[...] = dot_full(inverse[...], left)
            return spread * spread

        lax.while_loop(lambda spread: spread > 1e-4, step, jnp.max(spread))
        answer[...] = dot_full(right[...], inverse[...])
        for _ in range(3):
            left = right[...] - dot_full(answer[...], gram[...])
            answer[...] = answer[...] + dot_full(left, inverse[...])

    coefficient_t = answer[...].astype(BF16)
    coefficient = answer[...].T.astype(BF16)
    fitted = dot(coefficient_t, panel[...])
    residual = (fitted - maps.astype(F32)).astype(BF16)
    pushed = dot(coefficient, residual)
    gradient = jnp.where(valid, 2.0 * pushed, 0.0).astype(BF16)
    for k in range(peers):
        for y in range(ny):
            outs[k][y] = gradient[k * share : (k + 1) * share, y * LANES : (y + 1) * LANES]


def fit(mask, density, section, blocks, parts, peers):
    pixels = blocks[0].shape[2]
    channels = sum(block.shape[1] for block in blocks)
    classes = density.shape[1]
    ny = pixels // LANES

    def one(block):
        at = section if block.shape[0] > 1 else 0
        return pl.BlockSpec((1,) + block.shape[1:], lambda i: (at, 0, 0))

    out = (ny, channels // peers, LANES)
    return pl.pallas_call(
        functools.partial(fit_kernel, parts, peers),
        grid=(1,),
        out_shape=[jax.ShapeDtypeStruct(out, BF16)] * peers,
        in_specs=[
            pl.BlockSpec((1, 1, pixels), lambda i: (section, 0, 0)),
            pl.BlockSpec((1, classes, pixels), lambda i: (section, 0, 0)),
        ]
        + [one(block) for block in blocks],
        out_specs=[pl.BlockSpec(out, lambda i: (0, 0, 0))] * peers,
        scratch_shapes=[
            pltpu.VMEM((channels, pixels), BF16),
            pltpu.VMEM((channels, channels), F32),
            pltpu.VMEM((classes, channels), F32),
            pltpu.VMEM((channels, channels), F32),
            pltpu.VMEM((classes, channels), F32),
        ],
        compiler_params=params(24),
        cost_estimate=cost(COST_F),
        name="fit",
    )(mask, density, *blocks)


def place_kernel(per, which, slots, *refs):
    blocks, (out, sems) = refs[: len(which)], refs[-2:]
    me = lax.axis_index(("gy", "af"))
    first = lax.axis_index("gz") * out.shape[0]
    copies = []
    for i, (k, section) in enumerate(which):
        z = slots[(me ^ k) * per + section] - first
        copies.append(pltpu.make_async_copy(blocks[i], out.at[z], sems.at[i]))
    for copy in copies:
        copy.start()
    for copy in copies:
        copy.wait()


def place(slots, returned, which, earlier, rows, per):
    blocks = [returned[key] for key in which]
    extra = [] if earlier is None else [earlier]
    return pl.pallas_call(
        functools.partial(place_kernel, per, which),
        out_shape=jax.ShapeDtypeStruct((rows,) + blocks[0].shape, BF16),
        in_specs=[spec(pltpu.SMEM)]
        + [spec(pltpu.VMEM)] * len(blocks)
        + [spec(pl.ANY)] * len(extra),
        out_specs=spec(pl.ANY),
        scratch_shapes=[pltpu.SemaphoreType.DMA((len(blocks),))],
        input_output_aliases={1 + len(blocks): 0} if extra else {},
        compiler_params=params(8),
        cost_estimate=cost(COST_P),
        name="place",
    )(slots, *blocks, *extra)


def body(atlas_features, velocity, section_density, pixel_mask, section_slice):
    rows, channels = atlas_features.shape[:2]
    slabs = lax.axis_size("gz")
    peers = lax.axis_size(("gy", "af"))
    per = section_density.shape[0]
    widths = WIDTHS if sum(WIDTHS) == channels else (channels,)
    chunks = len(widths)

    atlas = jnp.transpose(atlas_features, (0, 2, 1, 3))
    vel = jnp.transpose(velocity, (0, 2, 1, 3))
    mask = pixel_mask.reshape(per, 1, -1)
    slots = section_slice

    edges = pack(atlas, vel, widths[0], 0)
    ones = [(i, i ^ 1) for i in range(slabs)]
    twos = [(i, i + 1) for i in range(1, slabs - 1, 2)]
    twos += [(j, i) for i, j in twos]
    own, _ = lax.optimization_barrier((atlas, edges[0]))
    levels = inner(own, vel)
    halos = []
    for part in range(chunks):
        if part > 0:
            later, _ = lax.optimization_barrier((atlas, edges[0]))
            edges = pack(later, vel, widths[part], sum(widths[:part]))
        one = lax.ppermute(edges[0], "gz", ones)
        two = lax.ppermute(edges[1], "gz", twos)
        halos.append((one, two))

    def swap(block, k):
        if k == 0:
            return block
        return lax.ppermute(block, ("gy", "af"), [(i, i ^ k) for i in range(peers)])

    arrived = {}
    start = 0
    for part, width in enumerate(widths):
        joined = part < chunks - 1
        one, two = halos[part]
        if part > 0:
            one, _ = lax.optimization_barrier((one, moved[0]))
        done = first_side(atlas, vel, one, halos[0][0], levels, width, start)
        moved = second_side(
            slots, atlas, vel, two, halos[0][1], levels, done, width, start, peers, per, joined
        )
        start += width
        if part > 0:
            moved, waiting, _ = lax.optimization_barrier(
                (moved, waiting, arrived[0, peers // 2, part - 1])
            )
            waiting = swap(waiting, 1)
            for section in range(per):
                arrived[section, 1, part - 1] = waiting
        for s in range(1 if joined else per):
            for k in reversed(range(peers)):
                block = moved[k if joined else k * per + s]
                if joined and k == 1:
                    waiting = block
                    continue
                block = swap(block, k)
                for section in range(per) if joined else [s]:
                    arrived[section, k, part] = block

    returned = {}
    for s in range(per):
        blocks = [arrived[s, k, part] for k in range(peers) for part in range(chunks)]
        gradients = fit(mask, section_density, s, blocks, chunks, peers)
        for k in range(peers):
            returned[k, s] = swap(gradients[k], k)
    last = per - 1
    early = [key for key in returned if key[1] < last or key[0] < peers // 2]
    late = [(k, last) for k in range(peers // 2, peers - 1)]
    result = place(slots, returned, early, None, rows, per)
    result = place(slots, returned, late, result, rows, per)
    result = place(slots, returned, [(peers - 1, last)], result, rows, per)
    return jnp.transpose(result, (0, 2, 1, 3))


def solution(mesh):
    return jax.shard_map(
        body,
        mesh=mesh,
        in_specs=(
            P(("groups", "gz"), ("gy", "af"), None, None),
            P(None, ("groups", "gz"), None, None),
            P(("groups", "gz", "gy", "af"), None, None),
            P(("groups", "gz", "gy", "af"), None),
            P(("groups", "gz")),
        ),
        out_specs=P(("groups", "gz"), ("gy", "af"), None, None),
        check_vma=False,
    )
```

```python
import functools
import itertools

import jax
import jax.numpy as jnp
from jax import lax
from jax.experimental import pallas as pl
from jax.experimental.pallas import tpu as pltpu
from jax.sharding import PartitionSpec as P

TSTEPS = 4
RATE = 0.04
RIDGE = 0.25
LANES = 128
F32 = jnp.float32
BF16 = jnp.bfloat16
VEL_ROWS = 16
WIDTHS = (32, 32)
COST_I, COST_T, COST_F, COST_P = 4 * 10**9, 10**9, 3 * 10**9, 15 * 10**8
EASY = 1.08
FAIR = 3.8


def spec(memory_space):
    return pl.BlockSpec(memory_space=memory_space)


def cost(count):
    return pl.CostEstimate(flops=count, bytes_accessed=0, transcendentals=0)


def params(mib):
    return pltpu.CompilerParams(vmem_limit_bytes=mib << 20)


def odd_slab():
    return lax.rem(lax.axis_index("gz"), 2)


def pack_kernel(width, start, atlas, vel, low, high, held, boxes, sems):
    outs = (low, high)
    rows, ny = atlas.shape[:2]
    odd = odd_slab()
    slots = TSTEPS - 1
    copies = []
    count = itertools.count()

    def move(source, target):
        copies.append(pltpu.make_async_copy(source, target, sems.at[next(count)]))
        copies[-1].start()

    if start == 0:
        move(vel, held)
    for side in range(2):
        first = jnp.where(odd == side, rows - TSTEPS, 0)
        for step in range(TSTEPS):
            move(
                atlas.at[first + step, :, pl.ds(start, width), :],
                outs[side].at[:, pl.ds(step * width, width), :],
            )
    if start == 0:
        copies.pop(0).wait()
        speed = held[...].astype(F32)
        filler = jnp.zeros((ny, VEL_ROWS - 3 * slots, LANES), F32)
        edges = []
        for first in (0, rows - slots):
            lines = [speed[k, :, first : first + slots, :] for k in range(3)]
            edges.append(jnp.concatenate(lines + [filler], axis=1))
        for side in range(2):
            boxes[side] = jnp.where(odd == side, edges[1], edges[0]).astype(BF16)
            move(boxes.at[side], outs[side].at[:, pl.ds(TSTEPS * width, VEL_ROWS), :])
    for copy in copies:
        copy.wait()


def pack(atlas, vel, width, start):
    ny = atlas.shape[1]
    rows = TSTEPS * width + (VEL_ROWS if start == 0 else 0)
    return pl.pallas_call(
        functools.partial(pack_kernel, width, start),
        out_shape=[jax.ShapeDtypeStruct((ny, rows, LANES), BF16)] * 2,
        in_specs=[spec(pl.ANY)] * 2,
        out_specs=[spec(pl.ANY)] * 2,
        scratch_shapes=[
            pltpu.VMEM(vel.shape, BF16),
            pltpu.VMEM((2, ny, VEL_ROWS, LANES), BF16),
            pltpu.SemaphoreType.DMA((2 * TSTEPS + 3,)),
        ],
        compiler_params=params(8),
        name="pack_edges",
    )(*(pltpu.with_memory_space_constraint(x, pltpu.HBM) for x in (atlas, vel)))


def set_weights(speed, coef, inside):
    lane = lax.broadcasted_iota(jnp.int32, (1,) + speed.shape[2:], 2)
    for y in range(speed.shape[1]):
        total = jnp.zeros(lane.shape, F32)
        for k in range(3):
            v = speed[k, y : y + 1]
            from_low = jnp.maximum(v, 0.0) + RATE
            from_high = RATE - jnp.minimum(v, 0.0)
            total = total + (from_low + from_high)
            if k == 2:
                from_low = jnp.where(lane == 0, 0.0, from_low)
                from_high = jnp.where(lane == LANES - 1, 0.0, from_high)
            coef[2 * k + 1, y : y + 1] = jnp.where(inside, from_low, 0.0)
            coef[2 * k + 2, y : y + 1] = jnp.where(inside, from_high, 0.0)
        coef[0, y : y + 1] = jnp.where(inside, 1.0 - total, 0.0)


def advance(coef, source, target, z, shift=0):
    at = z - shift
    ny = source.shape[1]
    for y in range(ny):
        weight = [coef[i, y, pl.ds(z, 1), :] for i in range(7)]
        center = source[at, y]
        total = weight[0] * center
        total = total + weight[1] * source[at - 1, y]
        total = total + weight[2] * source[at + 1, y]
        if y > 0:
            total = total + weight[3] * source[at, y - 1]
        if y < ny - 1:
            total = total + weight[4] * source[at, y + 1]
        total = total + weight[5] * pltpu.roll(center, 1, axis=1)
        total = total + weight[6] * pltpu.roll(center, LANES - 1, axis=1)
        target[z, y] = total


def advance_pairs(coef, source, target, pairs, first, shift=0):
    def step(i, carry):
        z = first(i)
        advance(coef, source, target, z, shift)
        advance(coef, source, target, z + 1, shift)
        return carry

    lax.fori_loop(0, pairs, step, 0)


def inner_kernel(atlas, vel, one, two, three, state, speed, coef):
    rows = atlas.shape[0]
    speed[...] = vel[...].astype(F32)
    set_weights(speed, coef, True)

    def load(z, carry):
        state[z] = atlas[z].astype(F32)
        return carry

    lax.fori_loop(0, rows, load, 0)
    levels = (state, one, two, three)
    for step in range(TSTEPS - 1):
        pairs = (rows - 2 * (step + 1)) // 2
        first = step + 1
        advance_pairs(coef, levels[step], levels[step + 1], pairs, lambda i: first + 2 * i)


def inner(atlas, vel):
    level = jax.ShapeDtypeStruct(atlas.shape, F32)
    return pl.pallas_call(
        inner_kernel,
        out_shape=[level] * (TSTEPS - 1),
        in_specs=[spec(pltpu.VMEM)] * 2,
        out_specs=[spec(pltpu.VMEM)] * (TSTEPS - 1),
        scratch_shapes=[
            pltpu.VMEM(atlas.shape, F32),
            pltpu.VMEM(vel.shape, F32),
            pltpu.VMEM((7,) + vel.shape[1:], F32),
        ],
        compiler_params=params(24),
        cost_estimate=cost(COST_I),
        name="inner_steps",
    )(atlas, vel)


def side_weights(high, vel, halo, speed, coef):
    rows, deep = vel.shape[2], coef.shape[2]
    edge = TSTEPS - 1
    slab, slabs = lax.axis_index("gz"), lax.axis_size("gz")
    has = jnp.where(high, slab < slabs - 1, slab > 0)
    beyond = halo[:, halo.shape[1] - VEL_ROWS :, :].astype(F32)
    for k in range(3):
        lines = beyond[:, edge * k : edge * (k + 1), :]
        speed[k, :, TSTEPS : TSTEPS + rows, :] = vel[k].astype(F32)
        speed[k, :, 1:TSTEPS, :] = lines
        speed[k, :, TSTEPS + rows : TSTEPS + rows + edge, :] = lines
    place = lax.broadcasted_iota(jnp.int32, (1, deep, LANES), 1)
    inside = ((place >= TSTEPS) & (place < TSTEPS + rows)) | has
    set_weights(speed, coef, inside & (place > 0) & (place < deep - 1))


def side_steps(high, width, start, atlas, halo, levels, state, coef):
    rows = atlas.shape[0]
    deep = rows + 2 * TSTEPS
    channels = slice(start, start + width)
    base = jnp.where(high, TSTEPS + rows, 0)
    for step in range(TSTEPS):
        state[0][base + step] = halo[:, step * width : (step + 1) * width, :].astype(F32)
    for i in range(2):
        z = jnp.where(high, rows - 2, 0) + i
        state[0][z + TSTEPS] = atlas[z, :, channels, :].astype(F32)
        for level in range(1, TSTEPS):
            z = jnp.where(high, rows - 2 - level, level) + i
            state[level][z + TSTEPS] = levels[level - 1][z, :, channels, :]
    for step in range(TSTEPS):
        first = jnp.where(high, deep - 5 - step, step + 1)
        target = state[(step + 1) % TSTEPS]
        for i in range(TSTEPS):
            advance(coef, state[step], target, first + i)


def first_kernel(width, start, atlas, vel, halo, *refs):
    levels, refs = refs[: TSTEPS - 1], refs[TSTEPS - 1 :]
    refs, state = refs[:-TSTEPS], refs[-TSTEPS:]
    high = odd_slab() == 0
    if start == 0:
        done, coef, speed = refs
        side_weights(high, vel, halo, speed, coef)
    else:
        coef, done = refs
    side_steps(high, width, start, atlas, halo, levels, state, coef)
    first = jnp.where(high, atlas.shape[0] - TSTEPS, 0)
    for i in range(TSTEPS):
        done[i] = state[0][first + TSTEPS + i].astype(BF16)


def second_kernel(peers, per, joined, width, start, slots, atlas, vel, halo, done, *refs):
    levels, refs = refs[: TSTEPS - 1], refs[TSTEPS - 1 :]
    refs, state = refs[:-TSTEPS], refs[-TSTEPS:]
    high = odd_slab() > 0
    if start == 0:
        outs, (coef, moved, speed) = refs[:-3], refs[-3:]
        side_weights(high, vel, halo, speed, coef)
    else:
        coef, outs, moved = refs[0], refs[1:-1], refs[-1]
    rows, ny = atlas.shape[:2]
    side_steps(high, width, start, atlas, halo, levels, state, coef)
    if rows > 2 * TSTEPS:
        source = levels[-1].at[:, :, start : start + width, :]
        pairs = (rows - 2 * TSTEPS) // 2
        advance_pairs(coef, source, state[0], pairs, lambda i: 2 * TSTEPS + 2 * i, TSTEPS)
        for z in range(TSTEPS, rows - TSTEPS):
            moved[z] = state[0][z + TSTEPS].astype(BF16)
    first = jnp.where(high, rows - TSTEPS, 0)
    other = rows - TSTEPS - first
    for i in range(TSTEPS):
        moved[first + i] = state[0][first + TSTEPS + i].astype(BF16)
        moved[other + i] = done[i]
    me = lax.axis_index(("gy", "af"))
    slab = lax.axis_index("gz")
    for k in range(peers):
        for s in range(per):
            z = slots[(me ^ k) * per + s] - slab * rows
            out = outs[k].at[s] if joined else outs[k * per + s].at[0]
            for y in range(ny):
                out[:, y * LANES : (y + 1) * LANES] = moved[z, y]


def side_shapes(atlas, width, start):
    rows, ny = atlas.shape[:2]
    deep = rows + 2 * TSTEPS
    scratch = [pltpu.VMEM((3, ny, deep, LANES), F32)] if start == 0 else []
    scratch += [pltpu.VMEM((deep, ny, width, LANES), F32)] * TSTEPS
    return jax.ShapeDtypeStruct((7, ny, deep, LANES), F32), scratch


def first_side(atlas, vel, halo, levels, coef, width, start):
    done = jax.ShapeDtypeStruct((TSTEPS, atlas.shape[1], width, LANES), BF16)
    weights, scratch = side_shapes(atlas, width, start)
    outs = [done, weights] if start == 0 else [done]
    extra = [] if start == 0 else [coef]
    result = pl.pallas_call(
        functools.partial(first_kernel, width, start),
        out_shape=outs,
        in_specs=[spec(pltpu.VMEM)] * (3 + len(levels) + len(extra)),
        out_specs=[spec(pltpu.VMEM)] * len(outs),
        scratch_shapes=scratch,
        compiler_params=params(28),
        cost_estimate=cost(COST_T),
        name="first_side",
    )(atlas, vel, halo, *levels, *extra)
    return result if start == 0 else (result[0], coef)


def second_side(slots, atlas, vel, halo, levels, done, coef, width, start, peers, per, joined):
    rows, ny = atlas.shape[:2]
    out = jax.ShapeDtypeStruct((per if joined else 1, width, ny * LANES), BF16)
    count = peers if joined else peers * per
    weights, scratch = side_shapes(atlas, width, start)
    outs = [out] * count + ([weights] if start == 0 else [])
    extra = [] if start == 0 else [coef]
    result = pl.pallas_call(
        functools.partial(second_kernel, peers, per, joined, width, start),
        out_shape=outs,
        in_specs=[spec(pltpu.SMEM)] + [spec(pltpu.VMEM)] * (4 + len(levels) + len(extra)),
        out_specs=[spec(pltpu.VMEM)] * len(outs),
        scratch_shapes=[pltpu.VMEM((rows, ny, width, LANES), BF16)] + scratch,
        compiler_params=params(28),
        cost_estimate=cost(COST_T),
        name="second_side",
    )(slots, atlas, vel, halo, done, *levels, *extra)
    return (result[:count], result[count]) if start == 0 else (result, coef)


def dot(a, b):
    return jnp.dot(a, b, preferred_element_type=F32)


def dot_full(a, b):
    return jnp.dot(a, b, preferred_element_type=F32, precision=lax.Precision.HIGHEST)


def halves(value):
    high = value.astype(BF16)
    return high, (value - high.astype(F32)).astype(BF16)


def fit_kernel(parts, peers, mask, density, *refs):
    blocks = refs[: parts * peers]
    outs = refs[parts * peers : parts * peers + peers]
    panel, gram, right, inverse, answer = refs[parts * peers + peers :]
    pixels = panel.shape[1]
    channels = panel.shape[0]
    share = channels // peers
    ny = pixels // LANES
    for k in range(peers):
        first = k * share
        for block in blocks[k * parts : (k + 1) * parts]:
            panel[first : first + block.shape[1], :] = block[0]
            first += block.shape[1]
    valid = mask[0] > 0
    every = panel[...]
    maps = density[0]
    masked = jnp.where(valid, every, jnp.zeros_like(every))
    contract = (((1,), (1,)), ((), ()))
    row = lax.broadcasted_iota(jnp.int32, (channels, channels), 0)
    column = lax.broadcasted_iota(jnp.int32, (channels, channels), 1)
    same = row == column
    gram[...] = lax.dot_general(every, masked, contract, preferred_element_type=F32) * (
        1.0 / pixels
    ) + jnp.where(same, RIDGE, 0.0)
    right[...] = lax.dot_general(maps, masked, contract, preferred_element_type=F32) * (
        1.0 / pixels
    )
    sums = jnp.sum(jnp.abs(gram[...]), axis=0, keepdims=True)
    bound_row = jnp.max(sums, axis=1, keepdims=True)
    bound = jnp.max(sums)
    start = 2.0 / (RIDGE + bound_row)
    spread = (bound_row - RIDGE) / (bound_row + RIDGE)

    def narrowed(spread):
        square = spread * spread
        return square / (2.0 - square), 2.0 / (2.0 - square)

    def doubled(scale):
        low = inverse[...].astype(BF16)
        left = jnp.where(same, 1.0, 0.0) - dot(gram[...].astype(BF16), low)
        inverse[...] = scale * (inverse[...] + dot(low, left.astype(BF16)))

    def refined():
        high, rest = halves(answer[...])
        gram_high, gram_rest = halves(gram[...])
        product = dot(high, gram_high) + (dot(rest, gram_high) + dot(high, gram_rest))
        left = (right[...] - product).astype(BF16)
        answer[...] = answer[...] + dot(left, inverse[...].astype(BF16))

    @pl.when(bound <= FAIR)
    def _():
        spread1, scale1 = narrowed(spread)
        spread2, scale2 = narrowed(spread1)
        _, scale3 = narrowed(spread2)
        inverse[...] = scale1 * (
            jnp.where(same, 2.0 * start, 0.0) - (start * start) * gram[...]
        )
        doubled(scale2)

        @pl.when(bound > EASY)
        def _():
            doubled(scale3)

        answer[...] = dot(right[...].astype(BF16), inverse[...].astype(BF16))
        refined()
        refined()

        @pl.when(bound > EASY)
        def _():
            refined()

    @pl.when(bound > FAIR)
    def _():
        inverse[...] = jnp.where(same, start, 0.0)

        def step(spread):
            left = jnp.where(same, 2.0, 0.0) - dot_full(gram[...], inverse[...])
            inverse[...] = dot_full(inverse[...], left)
            return spread * spread

        lax.while_loop(lambda spread: spread > 1e-4, step, jnp.max(spread))
        answer[...] = dot_full(right[...], inverse[...])
        for _ in range(3):
            left = right[...] - dot_full(answer[...], gram[...])
            answer[...] = answer[...] + dot_full(left, inverse[...])

    coefficient_t = answer[...].astype(BF16)
    coefficient = answer[...].T.astype(BF16)
    fitted = dot(coefficient_t, panel[...])
    residual = (fitted - maps.astype(F32)).astype(BF16)
    pushed = dot(coefficient, residual)
    gradient = jnp.where(valid, 2.0 * pushed, 0.0).astype(BF16)
    for k in range(peers):
        for y in range(ny):
            outs[k][y] = gradient[k * share : (k + 1) * share, y * LANES : (y + 1) * LANES]


def fit(mask, density, section, blocks, parts, peers):
    pixels = blocks[0].shape[2]
    channels = sum(block.shape[1] for block in blocks)
    classes = density.shape[1]
    ny = pixels // LANES

    def one(block):
        at = section if block.shape[0] > 1 else 0
        return pl.BlockSpec((1,) + block.shape[1:], lambda i: (at, 0, 0))

    out = (ny, channels // peers, LANES)
    return pl.pallas_call(
        functools.partial(fit_kernel, parts, peers),
        grid=(1,),
        out_shape=[jax.ShapeDtypeStruct(out, BF16)] * peers,
        in_specs=[
            pl.BlockSpec((1, 1, pixels), lambda i: (section, 0, 0)),
            pl.BlockSpec((1, classes, pixels), lambda i: (section, 0, 0)),
        ]
        + [one(block) for block in blocks],
        out_specs=[pl.BlockSpec(out, lambda i: (0, 0, 0))] * peers,
        scratch_shapes=[
            pltpu.VMEM((channels, pixels), BF16),
            pltpu.VMEM((channels, channels), F32),
            pltpu.VMEM((classes, channels), F32),
            pltpu.VMEM((channels, channels), F32),
            pltpu.VMEM((classes, channels), F32),
        ],
        compiler_params=params(24),
        cost_estimate=cost(COST_F),
        name="fit",
    )(mask, density, *blocks)


def place_kernel(per, which, slots, *refs):
    blocks, (out, sems) = refs[: len(which)], refs[-2:]
    me = lax.axis_index(("gy", "af"))
    first = lax.axis_index("gz") * out.shape[0]
    copies = []
    for i, (k, section) in enumerate(which):
        z = slots[(me ^ k) * per + section] - first
        copies.append(pltpu.make_async_copy(blocks[i], out.at[z], sems.at[i]))
    for copy in copies:
        copy.start()
    for copy in copies:
        copy.wait()


def place(slots, returned, which, earlier, rows, per):
    blocks = [returned[key] for key in which]
    extra = [] if earlier is None else [earlier]
    return pl.pallas_call(
        functools.partial(place_kernel, per, which),
        out_shape=jax.ShapeDtypeStruct((rows,) + blocks[0].shape, BF16),
        in_specs=[spec(pltpu.SMEM)]
        + [spec(pltpu.VMEM)] * len(blocks)
        + [spec(pl.ANY)] * len(extra),
        out_specs=spec(pl.ANY),
        scratch_shapes=[pltpu.SemaphoreType.DMA((len(blocks),))],
        input_output_aliases={1 + len(blocks): 0} if extra else {},
        compiler_params=params(8),
        cost_estimate=cost(COST_P),
        name="place",
    )(slots, *blocks, *extra)


def body(atlas_features, velocity, section_density, pixel_mask, section_slice):
    rows, channels = atlas_features.shape[:2]
    slabs = lax.axis_size("gz")
    peers = lax.axis_size(("gy", "af"))
    per = section_density.shape[0]
    widths = WIDTHS if sum(WIDTHS) == channels else (channels,)
    chunks = len(widths)

    atlas = jnp.transpose(atlas_features, (0, 2, 1, 3))
    vel = jnp.transpose(velocity, (0, 2, 1, 3))
    mask = pixel_mask.reshape(per, 1, -1)
    slots = section_slice

    edges = pack(atlas, vel, widths[0], 0)
    ones = [(i, i ^ 1) for i in range(slabs)]
    twos = [(i, i + 1) for i in range(1, slabs - 1, 2)]
    twos += [(j, i) for i, j in twos]
    own, _ = lax.optimization_barrier((atlas, edges[0]))
    levels = inner(own, vel)
    halos = []
    for part in range(chunks):
        if part > 0:
            later, _ = lax.optimization_barrier((atlas, edges[0]))
            edges = pack(later, vel, widths[part], sum(widths[:part]))
        one = lax.ppermute(edges[0], "gz", ones)
        two = lax.ppermute(edges[1], "gz", twos)
        halos.append((one, two))

    def swap(block, k):
        if k == 0:
            return block
        return lax.ppermute(block, ("gy", "af"), [(i, i ^ k) for i in range(peers)])

    arrived = {}
    coef_one = coef_two = None
    start = 0
    for part, width in enumerate(widths):
        joined = part < chunks - 1
        one, two = halos[part]
        if part > 0:
            one, _ = lax.optimization_barrier((one, moved[0]))
        done, coef_one = first_side(atlas, vel, one, levels, coef_one, width, start)
        moved, coef_two = second_side(
            slots, atlas, vel, two, levels, done, coef_two, width, start, peers, per, joined
        )
        start += width
        if part > 0:
            moved, waiting, _ = lax.optimization_barrier(
                (moved, waiting, arrived[0, peers // 2, part - 1])
            )
            waiting = swap(waiting, 1)
            for section in range(per):
                arrived[section, 1, part - 1] = waiting
        for s in range(1 if joined else per):
            for k in reversed(range(peers)):
                block = moved[k if joined else k * per + s]
                if joined and k == 1:
                    waiting = block
                    continue
                block = swap(block, k)
                for section in range(per) if joined else [s]:
                    arrived[section, k, part] = block

    returned = {}
    for s in range(per):
        blocks = [arrived[s, k, part] for k in range(peers) for part in range(chunks)]
        gradients = fit(mask, section_density, s, blocks, chunks, peers)
        for k in range(peers):
            returned[k, s] = swap(gradients[k], k)
    last = per - 1
    early = [key for key in returned if key[1] < last or key[0] < peers // 2]
    late = [(k, last) for k in range(peers // 2, peers - 1)]
    result = place(slots, returned, early, None, rows, per)
    result = place(slots, returned, late, result, rows, per)
    result = place(slots, returned, [(peers - 1, last)], result, rows, per)
    return jnp.transpose(result, (0, 2, 1, 3))


def solution(mesh):
    return jax.shard_map(
        body,
        mesh=mesh,
        in_specs=(
            P(("groups", "gz"), ("gy", "af"), None, None),
            P(None, ("groups", "gz"), None, None),
            P(("groups", "gz", "gy", "af"), None, None),
            P(("groups", "gz", "gy", "af"), None),
            P(("groups", "gz")),
        ),
        out_specs=P(("groups", "gz"), ("gy", "af"), None, None),
        check_vma=False,
    )
```

```python
import functools
import itertools

import jax
import jax.numpy as jnp
from jax import lax
from jax.experimental import pallas as pl
from jax.experimental.pallas import tpu as pltpu
from jax.sharding import PartitionSpec as P

TSTEPS = 4
RATE = 0.04
RIDGE = 0.25
LANES = 128
F32 = jnp.float32
BF16 = jnp.bfloat16
VEL_ROWS = 16
WIDTHS = (32, 32)
COST_I, COST_T, COST_F, COST_P = 4 * 10**9, 10**9, 3 * 10**9, 15 * 10**8
EASY = 1.08
FAIR = 3.8


def spec(memory_space):
    return pl.BlockSpec(memory_space=memory_space)


def cost(count):
    return pl.CostEstimate(flops=count, bytes_accessed=0, transcendentals=0)


def params(mib):
    return pltpu.CompilerParams(vmem_limit_bytes=mib << 20)


def odd_slab():
    return lax.rem(lax.axis_index("gz"), 2)


def pack_kernel(width, start, atlas, vel, low, high, held, boxes, sems):
    outs = (low, high)
    rows, ny = atlas.shape[:2]
    odd = odd_slab()
    slots = TSTEPS - 1
    copies = []
    count = itertools.count()

    def move(source, target):
        copies.append(pltpu.make_async_copy(source, target, sems.at[next(count)]))
        copies[-1].start()

    if start == 0:
        move(vel, held)
    for side in range(2):
        first = jnp.where(odd == side, rows - TSTEPS, 0)
        for step in range(TSTEPS):
            move(
                atlas.at[first + step, :, pl.ds(start, width), :],
                outs[side].at[:, pl.ds(step * width, width), :],
            )
    if start == 0:
        copies.pop(0).wait()
        speed = held[...].astype(F32)
        filler = jnp.zeros((ny, VEL_ROWS - 3 * slots, LANES), F32)
        edges = []
        for first in (0, rows - slots):
            lines = [speed[k, :, first : first + slots, :] for k in range(3)]
            edges.append(jnp.concatenate(lines + [filler], axis=1))
        for side in range(2):
            boxes[side] = jnp.where(odd == side, edges[1], edges[0]).astype(BF16)
            move(boxes.at[side], outs[side].at[:, pl.ds(TSTEPS * width, VEL_ROWS), :])
    for copy in copies:
        copy.wait()


def pack(atlas, vel, width, start):
    ny = atlas.shape[1]
    rows = TSTEPS * width + (VEL_ROWS if start == 0 else 0)
    return pl.pallas_call(
        functools.partial(pack_kernel, width, start),
        out_shape=[jax.ShapeDtypeStruct((ny, rows, LANES), BF16)] * 2,
        in_specs=[spec(pl.ANY)] * 2,
        out_specs=[spec(pl.ANY)] * 2,
        scratch_shapes=[
            pltpu.VMEM(vel.shape, BF16),
            pltpu.VMEM((2, ny, VEL_ROWS, LANES), BF16),
            pltpu.SemaphoreType.DMA((2 * TSTEPS + 3,)),
        ],
        compiler_params=params(8),
        name="pack_edges",
    )(*(pltpu.with_memory_space_constraint(x, pltpu.HBM) for x in (atlas, vel)))


def set_weights(speed, coef, inside):
    lane = lax.broadcasted_iota(jnp.int32, (1,) + speed.shape[2:], 2)
    for y in range(speed.shape[1]):
        total = jnp.zeros(lane.shape, F32)
        for k in range(3):
            v = speed[k, y : y + 1]
            from_low = jnp.maximum(v, 0.0) + RATE
            from_high = RATE - jnp.minimum(v, 0.0)
            total = total + (from_low + from_high)
            if k == 2:
                from_low = jnp.where(lane == 0, 0.0, from_low)
                from_high = jnp.where(lane == LANES - 1, 0.0, from_high)
            coef[2 * k + 1, y : y + 1] = jnp.where(inside, from_low, 0.0)
            coef[2 * k + 2, y : y + 1] = jnp.where(inside, from_high, 0.0)
        coef[0, y : y + 1] = jnp.where(inside, 1.0 - total, 0.0)


def advance(coef, source, target, z, shift=0):
    at = z - shift
    ny = source.shape[1]
    for y in range(ny):
        weight = [coef[i, y, pl.ds(z, 1), :] for i in range(7)]
        center = source[at, y]
        total = weight[0] * center
        total = total + weight[1] * source[at - 1, y]
        total = total + weight[2] * source[at + 1, y]
        if y > 0:
            total = total + weight[3] * source[at, y - 1]
        if y < ny - 1:
            total = total + weight[4] * source[at, y + 1]
        total = total + weight[5] * pltpu.roll(center, 1, axis=1)
        total = total + weight[6] * pltpu.roll(center, LANES - 1, axis=1)
        target[z, y] = total


def advance_pairs(coef, source, target, pairs, first, shift=0):
    def step(i, carry):
        z = first(i)
        advance(coef, source, target, z, shift)
        advance(coef, source, target, z + 1, shift)
        return carry

    lax.fori_loop(0, pairs, step, 0)


def inner_kernel(atlas, vel, one, two, three, state, speed, coef):
    rows = atlas.shape[0]
    speed[...] = vel[...].astype(F32)
    set_weights(speed, coef, True)

    def load(z, carry):
        state[z] = atlas[z].astype(F32)
        return carry

    lax.fori_loop(0, rows, load, 0)
    levels = (state, one, two, three)
    for step in range(TSTEPS - 1):
        pairs = (rows - 2 * (step + 1)) // 2
        first = step + 1
        advance_pairs(coef, levels[step], levels[step + 1], pairs, lambda i: first + 2 * i)


def inner(atlas, vel):
    level = jax.ShapeDtypeStruct(atlas.shape, F32)
    return pl.pallas_call(
        inner_kernel,
        out_shape=[level] * (TSTEPS - 1),
        in_specs=[spec(pltpu.VMEM)] * 2,
        out_specs=[spec(pltpu.VMEM)] * (TSTEPS - 1),
        scratch_shapes=[
            pltpu.VMEM(atlas.shape, F32),
            pltpu.VMEM(vel.shape, F32),
            pltpu.VMEM((7,) + vel.shape[1:], F32),
        ],
        compiler_params=params(24),
        cost_estimate=cost(COST_I),
        name="inner_steps",
    )(atlas, vel)


def side_weights(high, vel, halo, speed, coef):
    rows, deep = vel.shape[2], coef.shape[2]
    edge = TSTEPS - 1
    slab, slabs = lax.axis_index("gz"), lax.axis_size("gz")
    has = jnp.where(high, slab < slabs - 1, slab > 0)
    beyond = halo[:, halo.shape[1] - VEL_ROWS :, :].astype(F32)
    for k in range(3):
        lines = beyond[:, edge * k : edge * (k + 1), :]
        speed[k, :, TSTEPS : TSTEPS + rows, :] = vel[k].astype(F32)
        speed[k, :, 1:TSTEPS, :] = lines
        speed[k, :, TSTEPS + rows : TSTEPS + rows + edge, :] = lines
    place = lax.broadcasted_iota(jnp.int32, (1, deep, LANES), 1)
    inside = ((place >= TSTEPS) & (place < TSTEPS + rows)) | has
    set_weights(speed, coef, inside & (place > 0) & (place < deep - 1))


def side_steps(high, width, start, atlas, halo, levels, state, coef):
    rows = atlas.shape[0]
    deep = rows + 2 * TSTEPS
    channels = slice(start, start + width)
    base = jnp.where(high, TSTEPS + rows, 0)
    for step in range(TSTEPS):
        state[0][base + step] = halo[:, step * width : (step + 1) * width, :].astype(F32)
    for i in range(2):
        z = jnp.where(high, rows - 2, 0) + i
        state[0][z + TSTEPS] = atlas[z, :, channels, :].astype(F32)
        for level in range(1, TSTEPS):
            z = jnp.where(high, rows - 2 - level, level) + i
            state[level][z + TSTEPS] = levels[level - 1][z, :, channels, :]
    for step in range(TSTEPS):
        first = jnp.where(high, deep - 5 - step, step + 1)
        target = state[(step + 1) % TSTEPS]
        for i in range(TSTEPS):
            advance(coef, state[step], target, first + i)


def first_kernel(width, start, atlas, vel, halo, *refs):
    levels, refs = refs[: TSTEPS - 1], refs[TSTEPS - 1 :]
    refs, state = refs[:-TSTEPS], refs[-TSTEPS:]
    high = odd_slab() == 0
    if start == 0:
        done, coef, speed = refs
        side_weights(high, vel, halo, speed, coef)
    else:
        coef, done = refs
    side_steps(high, width, start, atlas, halo, levels, state, coef)
    first = jnp.where(high, atlas.shape[0] - TSTEPS, 0)
    for i in range(TSTEPS):
        done[i] = state[0][first + TSTEPS + i].astype(BF16)


def second_kernel(peers, per, joined, width, start, slots, atlas, vel, halo, done, *refs):
    levels, refs, (order, sem) = refs[: TSTEPS - 1], refs[TSTEPS - 1 : -2], refs[-2:]
    refs, state = refs[:-TSTEPS], refs[-TSTEPS:]
    fetch = pltpu.make_async_copy(slots, order, sem)
    fetch.start()
    high = odd_slab() > 0
    if start == 0:
        outs, (coef, moved, speed) = refs[:-3], refs[-3:]
        side_weights(high, vel, halo, speed, coef)
    else:
        coef, outs, moved = refs[0], refs[1:-1], refs[-1]
    rows, ny = atlas.shape[:2]
    side_steps(high, width, start, atlas, halo, levels, state, coef)
    if rows > 2 * TSTEPS:
        source = levels[-1].at[:, :, start : start + width, :]
        pairs = (rows - 2 * TSTEPS) // 2
        advance_pairs(coef, source, state[0], pairs, lambda i: 2 * TSTEPS + 2 * i, TSTEPS)
        for z in range(TSTEPS, rows - TSTEPS):
            moved[z] = state[0][z + TSTEPS].astype(BF16)
    first = jnp.where(high, rows - TSTEPS, 0)
    other = rows - TSTEPS - first
    for i in range(TSTEPS):
        moved[first + i] = state[0][first + TSTEPS + i].astype(BF16)
        moved[other + i] = done[i]
    me = lax.axis_index(("gy", "af"))
    slab = lax.axis_index("gz")
    fetch.wait()
    for k in range(peers):
        for s in range(per):
            z = order[(me ^ k) * per + s] - slab * rows
            out = outs[k].at[s] if joined else outs[k * per + s].at[0]
            out[...] = moved[z]


def side_shapes(atlas, width, start):
    rows, ny = atlas.shape[:2]
    deep = rows + 2 * TSTEPS
    scratch = [pltpu.VMEM((3, ny, deep, LANES), F32)] if start == 0 else []
    scratch += [pltpu.VMEM((deep, ny, width, LANES), F32)] * TSTEPS
    return jax.ShapeDtypeStruct((7, ny, deep, LANES), F32), scratch


def first_side(atlas, vel, halo, levels, coef, width, start):
    done = jax.ShapeDtypeStruct((TSTEPS, atlas.shape[1], width, LANES), BF16)
    weights, scratch = side_shapes(atlas, width, start)
    outs = [done, weights] if start == 0 else [done]
    extra = [] if start == 0 else [coef]
    result = pl.pallas_call(
        functools.partial(first_kernel, width, start),
        out_shape=outs,
        in_specs=[spec(pltpu.VMEM)] * (3 + len(levels) + len(extra)),
        out_specs=[spec(pltpu.VMEM)] * len(outs),
        scratch_shapes=scratch,
        compiler_params=params(28),
        cost_estimate=cost(COST_T),
        name="first_side",
    )(atlas, vel, halo, *levels, *extra)
    return result if start == 0 else (result[0], coef)


def second_side(slots, atlas, vel, halo, levels, done, coef, width, start, peers, per, joined):
    rows, ny = atlas.shape[:2]
    out = jax.ShapeDtypeStruct((per if joined else 1, ny, width, LANES), BF16)
    count = peers if joined else peers * per
    weights, scratch = side_shapes(atlas, width, start)
    outs = [out] * count + ([weights] if start == 0 else [])
    extra = [] if start == 0 else [coef]
    result = pl.pallas_call(
        functools.partial(second_kernel, peers, per, joined, width, start),
        out_shape=outs,
        in_specs=[spec(pl.ANY)] + [spec(pltpu.VMEM)] * (4 + len(levels) + len(extra)),
        out_specs=[spec(pltpu.VMEM)] * len(outs),
        scratch_shapes=[pltpu.VMEM((rows, ny, width, LANES), BF16)]
        + scratch
        + [pltpu.SMEM((rows,), jnp.int32), pltpu.SemaphoreType.DMA],
        compiler_params=params(28),
        cost_estimate=cost(COST_T),
        name="second_side",
    )(slots, atlas, vel, halo, done, *levels, *extra)
    return (result[:count], result[count]) if start == 0 else (result, coef)


def dot(a, b):
    return jnp.dot(a, b, preferred_element_type=F32)


def dot_full(a, b):
    return jnp.dot(a, b, preferred_element_type=F32, precision=lax.Precision.HIGHEST)


def halves(value):
    high = value.astype(BF16)
    return high, (value - high.astype(F32)).astype(BF16)


def fit_kernel(parts, peers, mask, density, *refs):
    blocks = refs[: parts * peers]
    outs = refs[parts * peers : parts * peers + peers]
    panel, gram, right, inverse, answer = refs[parts * peers + peers :]
    pixels = panel.shape[1]
    channels = panel.shape[0]
    share = channels // peers
    ny = pixels // LANES
    for k in range(peers):
        first = k * share
        for block in blocks[k * parts : (k + 1) * parts]:
            for y in range(ny):
                rows = slice(first, first + block.shape[2])
                panel[rows, y * LANES : (y + 1) * LANES] = block[0, y]
            first += block.shape[2]
    valid = mask[0] > 0
    every = panel[...]
    maps = density[0]
    masked = jnp.where(valid, every, jnp.zeros_like(every))
    contract = (((1,), (1,)), ((), ()))
    row = lax.broadcasted_iota(jnp.int32, (channels, channels), 0)
    column = lax.broadcasted_iota(jnp.int32, (channels, channels), 1)
    same = row == column
    gram[...] = lax.dot_general(every, masked, contract, preferred_element_type=F32) * (
        1.0 / pixels
    ) + jnp.where(same, RIDGE, 0.0)
    right[...] = lax.dot_general(maps, masked, contract, preferred_element_type=F32) * (
        1.0 / pixels
    )
    sums = jnp.sum(jnp.abs(gram[...]), axis=0, keepdims=True)
    bound_row = jnp.max(sums, axis=1, keepdims=True)
    bound = jnp.max(sums)
    start = 2.0 / (RIDGE + bound_row)
    spread = (bound_row - RIDGE) / (bound_row + RIDGE)

    def narrowed(spread):
        square = spread * spread
        return square / (2.0 - square), 2.0 / (2.0 - square)

    def doubled(scale):
        low = inverse[...].astype(BF16)
        left = jnp.where(same, 1.0, 0.0) - dot(gram[...].astype(BF16), low)
        inverse[...] = scale * (inverse[...] + dot(low, left.astype(BF16)))

    def refined():
        high, rest = halves(answer[...])
        gram_high, gram_rest = halves(gram[...])
        product = dot(high, gram_high) + (dot(rest, gram_high) + dot(high, gram_rest))
        left = (right[...] - product).astype(BF16)
        answer[...] = answer[...] + dot(left, inverse[...].astype(BF16))

    @pl.when(bound <= FAIR)
    def _():
        spread1, scale1 = narrowed(spread)
        spread2, scale2 = narrowed(spread1)
        _, scale3 = narrowed(spread2)
        inverse[...] = scale1 * (
            jnp.where(same, 2.0 * start, 0.0) - (start * start) * gram[...]
        )
        doubled(scale2)

        @pl.when(bound > EASY)
        def _():
            doubled(scale3)

        answer[...] = dot(right[...].astype(BF16), inverse[...].astype(BF16))
        refined()
        refined()

        @pl.when(bound > EASY)
        def _():
            refined()

    @pl.when(bound > FAIR)
    def _():
        inverse[...] = jnp.where(same, start, 0.0)

        def step(spread):
            left = jnp.where(same, 2.0, 0.0) - dot_full(gram[...], inverse[...])
            inverse[...] = dot_full(inverse[...], left)
            return spread * spread

        lax.while_loop(lambda spread: spread > 1e-4, step, jnp.max(spread))
        answer[...] = dot_full(right[...], inverse[...])
        for _ in range(3):
            left = right[...] - dot_full(answer[...], gram[...])
            answer[...] = answer[...] + dot_full(left, inverse[...])

    coefficient_t = answer[...].astype(BF16)
    coefficient = answer[...].T.astype(BF16)
    fitted = dot(coefficient_t, panel[...])
    residual = (fitted - maps.astype(F32)).astype(BF16)
    pushed = dot(coefficient, residual)
    gradient = jnp.where(valid, 2.0 * pushed, 0.0).astype(BF16)
    for k in range(peers):
        for y in range(ny):
            outs[k][y] = gradient[k * share : (k + 1) * share, y * LANES : (y + 1) * LANES]


def fit(mask, density, section, blocks, parts, peers):
    ny = blocks[0].shape[1]
    pixels = ny * LANES
    channels = sum(block.shape[2] for block in blocks)
    classes = density.shape[1]

    def one(block):
        at = section if block.shape[0] > 1 else 0
        return pl.BlockSpec((1,) + block.shape[1:], lambda i: (at, 0, 0, 0))

    out = (ny, channels // peers, LANES)
    return pl.pallas_call(
        functools.partial(fit_kernel, parts, peers),
        grid=(1,),
        out_shape=[jax.ShapeDtypeStruct(out, BF16)] * peers,
        in_specs=[
            pl.BlockSpec((1, 1, pixels), lambda i: (section, 0, 0)),
            pl.BlockSpec((1, classes, pixels), lambda i: (section, 0, 0)),
        ]
        + [one(block) for block in blocks],
        out_specs=[pl.BlockSpec(out, lambda i: (0, 0, 0))] * peers,
        scratch_shapes=[
            pltpu.VMEM((channels, pixels), BF16),
            pltpu.VMEM((channels, channels), F32),
            pltpu.VMEM((classes, channels), F32),
            pltpu.VMEM((channels, channels), F32),
            pltpu.VMEM((classes, channels), F32),
        ],
        compiler_params=params(24),
        cost_estimate=cost(COST_F),
        name="fit",
    )(mask, density, *blocks)


def place_kernel(per, which, slots, *refs):
    blocks, (out, sems) = refs[: len(which)], refs[-2:]
    me = lax.axis_index(("gy", "af"))
    first = lax.axis_index("gz") * out.shape[0]
    copies = []
    for i, (k, section) in enumerate(which):
        z = slots[(me ^ k) * per + section] - first
        copies.append(pltpu.make_async_copy(blocks[i], out.at[z], sems.at[i]))
    for copy in copies:
        copy.start()
    for copy in copies:
        copy.wait()


def place(slots, returned, which, earlier, rows, per):
    blocks = [returned[key] for key in which]
    extra = [] if earlier is None else [earlier]
    return pl.pallas_call(
        functools.partial(place_kernel, per, which),
        out_shape=jax.ShapeDtypeStruct((rows,) + blocks[0].shape, BF16),
        in_specs=[spec(pltpu.SMEM)]
        + [spec(pltpu.VMEM)] * len(blocks)
        + [spec(pl.ANY)] * len(extra),
        out_specs=spec(pl.ANY),
        scratch_shapes=[pltpu.SemaphoreType.DMA((len(blocks),))],
        input_output_aliases={1 + len(blocks): 0} if extra else {},
        compiler_params=params(8),
        cost_estimate=cost(COST_P),
        name="place",
    )(slots, *blocks, *extra)


def body(atlas_features, velocity, section_density, pixel_mask, section_slice):
    rows, channels = atlas_features.shape[:2]
    slabs = lax.axis_size("gz")
    peers = lax.axis_size(("gy", "af"))
    per = section_density.shape[0]
    widths = WIDTHS if sum(WIDTHS) == channels else (channels,)
    chunks = len(widths)

    atlas = jnp.transpose(atlas_features, (0, 2, 1, 3))
    vel = jnp.transpose(velocity, (0, 2, 1, 3))
    mask = pixel_mask.reshape(per, 1, -1)
    slots = section_slice

    edges = pack(atlas, vel, widths[0], 0)
    ones = [(i, i ^ 1) for i in range(slabs)]
    twos = [(i, i + 1) for i in range(1, slabs - 1, 2)]
    twos += [(j, i) for i, j in twos]
    own, _ = lax.optimization_barrier((atlas, edges[0]))
    levels = inner(own, vel)
    halos = []
    for part in range(chunks):
        if part > 0:
            later, _ = lax.optimization_barrier((atlas, edges[0]))
            edges = pack(later, vel, widths[part], sum(widths[:part]))
        one = lax.ppermute(edges[0], "gz", ones)
        two = lax.ppermute(edges[1], "gz", twos)
        halos.append((one, two))

    def swap(block, k):
        if k == 0:
            return block
        return lax.ppermute(block, ("gy", "af"), [(i, i ^ k) for i in range(peers)])

    arrived = {}
    coef_one = coef_two = None
    start = 0
    for part, width in enumerate(widths):
        joined = part < chunks - 1
        one, two = halos[part]
        if part > 0:
            one, _ = lax.optimization_barrier((one, moved[0]))
        done, coef_one = first_side(atlas, vel, one, levels, coef_one, width, start)
        moved, coef_two = second_side(
            slots, atlas, vel, two, levels, done, coef_two, width, start, peers, per, joined
        )
        start += width
        if part > 0:
            moved, waiting, _ = lax.optimization_barrier(
                (moved, waiting, arrived[0, peers // 2, part - 1])
            )
            waiting = swap(waiting, 1)
            for section in range(per):
                arrived[section, 1, part - 1] = waiting
        for s in range(1 if joined else per):
            for k in reversed(range(peers)):
                block = moved[k if joined else k * per + s]
                if joined and k == 1:
                    waiting = block
                    continue
                block = swap(block, k)
                for section in range(per) if joined else [s]:
                    arrived[section, k, part] = block

    returned = {}
    for s in range(per):
        blocks = [arrived[s, k, part] for k in range(peers) for part in range(chunks)]
        gradients = fit(mask, section_density, s, blocks, chunks, peers)
        for k in range(peers):
            returned[k, s] = swap(gradients[k], k)
    last = per - 1
    early = [key for key in returned if key[1] < last or key[0] < peers // 2]
    late = [(k, last) for k in range(peers // 2, peers - 1)]
    result = place(slots, returned, early, None, rows, per)
    result = place(slots, returned, late, result, rows, per)
    far = peers - 1
    at = (lax.axis_index(("gy", "af")) ^ far) * per + last
    at = lax.dynamic_index_in_dim(slots, at, keepdims=False) - lax.axis_index("gz") * rows
    result = lax.dynamic_update_slice(result, returned[far, last][None], (at, 0, 0, 0))
    return jnp.transpose(result, (0, 2, 1, 3))


def solution(mesh):
    return jax.shard_map(
        body,
        mesh=mesh,
        in_specs=(
            P(("groups", "gz"), ("gy", "af"), None, None),
            P(None, ("groups", "gz"), None, None),
            P(("groups", "gz", "gy", "af"), None, None),
            P(("groups", "gz", "gy", "af"), None),
            P(("groups", "gz")),
        ),
        out_specs=P(("groups", "gz"), ("gy", "af"), None, None),
        check_vma=False,
    )
```

```python
import functools
import itertools

import jax
import jax.numpy as jnp
from jax import lax
from jax.experimental import pallas as pl
from jax.experimental.pallas import tpu as pltpu
from jax.sharding import PartitionSpec as P

TSTEPS = 4
RATE = 0.04
RIDGE = 0.25
LANES = 128
F32 = jnp.float32
BF16 = jnp.bfloat16
VEL_ROWS = 16
WIDTHS = (32, 32)
COST_I, COST_T, COST_F, COST_P = 4 * 10**9, 10**8, 10 * 10**9, 10**8
EASY = 1.08
FAIR = 3.8


def spec(memory_space):
    return pl.BlockSpec(memory_space=memory_space)


def cost(count):
    return pl.CostEstimate(flops=count, bytes_accessed=0, transcendentals=0)


def params(mib):
    return pltpu.CompilerParams(vmem_limit_bytes=mib << 20)


def odd_slab():
    return lax.rem(lax.axis_index("gz"), 2)


def pack_kernel(width, start, atlas, vel, low, high, held, boxes, sems):
    outs = (low, high)
    rows, ny = atlas.shape[:2]
    odd = odd_slab()
    slots = TSTEPS - 1
    copies = []
    count = itertools.count()

    def move(source, target):
        copies.append(pltpu.make_async_copy(source, target, sems.at[next(count)]))
        copies[-1].start()

    if start == 0:
        move(vel, held)
    for side in range(2):
        first = jnp.where(odd == side, rows - TSTEPS, 0)
        for step in range(TSTEPS):
            move(
                atlas.at[first + step, :, pl.ds(start, width), :],
                outs[side].at[:, pl.ds(step * width, width), :],
            )
    if start == 0:
        copies.pop(0).wait()
        speed = held[...].astype(F32)
        filler = jnp.zeros((ny, VEL_ROWS - 3 * slots, LANES), F32)
        edges = []
        for first in (0, rows - slots):
            lines = [speed[k, :, first : first + slots, :] for k in range(3)]
            edges.append(jnp.concatenate(lines + [filler], axis=1))
        for side in range(2):
            boxes[side] = jnp.where(odd == side, edges[1], edges[0]).astype(BF16)
            move(boxes.at[side], outs[side].at[:, pl.ds(TSTEPS * width, VEL_ROWS), :])
    for copy in copies:
        copy.wait()


def pack(atlas, vel, width, start):
    ny = atlas.shape[1]
    rows = TSTEPS * width + (VEL_ROWS if start == 0 else 0)
    return pl.pallas_call(
        functools.partial(pack_kernel, width, start),
        out_shape=[jax.ShapeDtypeStruct((ny, rows, LANES), BF16)] * 2,
        in_specs=[spec(pl.ANY)] * 2,
        out_specs=[spec(pl.ANY)] * 2,
        scratch_shapes=[
            pltpu.VMEM(vel.shape, BF16),
            pltpu.VMEM((2, ny, VEL_ROWS, LANES), BF16),
            pltpu.SemaphoreType.DMA((2 * TSTEPS + 3,)),
        ],
        compiler_params=params(8),
        name="pack_edges",
    )(*(pltpu.with_memory_space_constraint(x, pltpu.HBM) for x in (atlas, vel)))


def set_weights(speed, coef, inside):
    lane = lax.broadcasted_iota(jnp.int32, (1,) + speed.shape[2:], 2)
    for y in range(speed.shape[1]):
        total = jnp.zeros(lane.shape, F32)
        for k in range(3):
            v = speed[k, y : y + 1]
            from_low = jnp.maximum(v, 0.0) + RATE
            from_high = RATE - jnp.minimum(v, 0.0)
            total = total + (from_low + from_high)
            if k == 2:
                from_low = jnp.where(lane == 0, 0.0, from_low)
                from_high = jnp.where(lane == LANES - 1, 0.0, from_high)
            coef[2 * k + 1, y : y + 1] = jnp.where(inside, from_low, 0.0)
            coef[2 * k + 2, y : y + 1] = jnp.where(inside, from_high, 0.0)
        coef[0, y : y + 1] = jnp.where(inside, 1.0 - total, 0.0)


def advance(coef, source, target, z, shift=0):
    at = z - shift
    ny = source.shape[1]
    for y in range(ny):
        weight = [coef[i, y, pl.ds(z, 1), :] for i in range(7)]
        center = source[at, y]
        total = weight[0] * center
        total = total + weight[1] * source[at - 1, y]
        total = total + weight[2] * source[at + 1, y]
        if y > 0:
            total = total + weight[3] * source[at, y - 1]
        if y < ny - 1:
            total = total + weight[4] * source[at, y + 1]
        total = total + weight[5] * pltpu.roll(center, 1, axis=1)
        total = total + weight[6] * pltpu.roll(center, LANES - 1, axis=1)
        target[z, y] = total


def advance_pairs(coef, source, target, pairs, first, shift=0):
    def step(i, carry):
        z = first(i)
        advance(coef, source, target, z, shift)
        advance(coef, source, target, z + 1, shift)
        return carry

    lax.fori_loop(0, pairs, step, 0)


def inner_kernel(atlas, vel, one, two, three, state, speed, coef):
    rows = atlas.shape[0]
    speed[...] = vel[...].astype(F32)
    set_weights(speed, coef, True)

    def load(z, carry):
        state[z] = atlas[z].astype(F32)
        return carry

    lax.fori_loop(0, rows, load, 0)
    levels = (state, one, two, three)
    for step in range(TSTEPS - 1):
        pairs = (rows - 2 * (step + 1)) // 2
        first = step + 1
        advance_pairs(coef, levels[step], levels[step + 1], pairs, lambda i: first + 2 * i)


def inner(atlas, vel):
    level = jax.ShapeDtypeStruct(atlas.shape, F32)
    return pl.pallas_call(
        inner_kernel,
        out_shape=[level] * (TSTEPS - 1),
        in_specs=[spec(pltpu.VMEM)] * 2,
        out_specs=[spec(pltpu.VMEM)] * (TSTEPS - 1),
        scratch_shapes=[
            pltpu.VMEM(atlas.shape, F32),
            pltpu.VMEM(vel.shape, F32),
            pltpu.VMEM((7,) + vel.shape[1:], F32),
        ],
        compiler_params=params(24),
        cost_estimate=cost(COST_I),
        name="inner_steps",
    )(atlas, vel)


def side_weights(high, vel, halo, speed, coef):
    rows, deep = vel.shape[2], coef.shape[2]
    edge = TSTEPS - 1
    slab, slabs = lax.axis_index("gz"), lax.axis_size("gz")
    has = jnp.where(high, slab < slabs - 1, slab > 0)
    beyond = halo[:, halo.shape[1] - VEL_ROWS :, :].astype(F32)
    for k in range(3):
        lines = beyond[:, edge * k : edge * (k + 1), :]
        speed[k, :, TSTEPS : TSTEPS + rows, :] = vel[k].astype(F32)
        speed[k, :, 1:TSTEPS, :] = lines
        speed[k, :, TSTEPS + rows : TSTEPS + rows + edge, :] = lines
    place = lax.broadcasted_iota(jnp.int32, (1, deep, LANES), 1)
    inside = ((place >= TSTEPS) & (place < TSTEPS + rows)) | has
    set_weights(speed, coef, inside & (place > 0) & (place < deep - 1))


def side_steps(high, width, start, atlas, halo, levels, state, coef):
    rows = atlas.shape[0]
    deep = rows + 2 * TSTEPS
    channels = slice(start, start + width)
    base = jnp.where(high, TSTEPS + rows, 0)
    for step in range(TSTEPS):
        state[0][base + step] = halo[:, step * width : (step + 1) * width, :].astype(F32)
    for i in range(2):
        z = jnp.where(high, rows - 2, 0) + i
        state[0][z + TSTEPS] = atlas[z, :, channels, :].astype(F32)
        for level in range(1, TSTEPS):
            z = jnp.where(high, rows - 2 - level, level) + i
            state[level][z + TSTEPS] = levels[level - 1][z, :, channels, :]
    for step in range(TSTEPS):
        first = jnp.where(high, deep - 5 - step, step + 1)
        target = state[(step + 1) % TSTEPS]
        for i in range(TSTEPS):
            advance(coef, state[step], target, first + i)


def first_kernel(width, start, atlas, vel, halo, *refs):
    levels, refs = refs[: TSTEPS - 1], refs[TSTEPS - 1 :]
    refs, state = refs[:-TSTEPS], refs[-TSTEPS:]
    high = odd_slab() == 0
    if start == 0:
        done, coef, speed = refs
        side_weights(high, vel, halo, speed, coef)
    else:
        coef, done = refs
    side_steps(high, width, start, atlas, halo, levels, state, coef)
    first = jnp.where(high, atlas.shape[0] - TSTEPS, 0)
    for i in range(TSTEPS):
        done[i] = state[0][first + TSTEPS + i].astype(BF16)


def second_kernel(peers, per, joined, width, start, slots, atlas, vel, halo, done, *refs):
    levels, refs, (order, sem) = refs[: TSTEPS - 1], refs[TSTEPS - 1 : -2], refs[-2:]
    refs, state = refs[:-TSTEPS], refs[-TSTEPS:]
    fetch = pltpu.make_async_copy(slots, order, sem)
    fetch.start()
    high = odd_slab() > 0
    if start == 0:
        outs, (coef, moved, speed) = refs[:-3], refs[-3:]
        side_weights(high, vel, halo, speed, coef)
    else:
        coef, outs, moved = refs[0], refs[1:-1], refs[-1]
    rows, ny = atlas.shape[:2]
    side_steps(high, width, start, atlas, halo, levels, state, coef)
    if rows > 2 * TSTEPS:
        source = levels[-1].at[:, :, start : start + width, :]
        pairs = (rows - 2 * TSTEPS) // 2
        advance_pairs(coef, source, state[0], pairs, lambda i: 2 * TSTEPS + 2 * i, TSTEPS)
        for z in range(TSTEPS, rows - TSTEPS):
            moved[z] = state[0][z + TSTEPS].astype(BF16)
    first = jnp.where(high, rows - TSTEPS, 0)
    other = rows - TSTEPS - first
    for i in range(TSTEPS):
        moved[first + i] = state[0][first + TSTEPS + i].astype(BF16)
        moved[other + i] = done[i]
    me = lax.axis_index(("gy", "af"))
    slab = lax.axis_index("gz")
    fetch.wait()
    for k in range(peers):
        for s in range(per):
            z = order[(me ^ k) * per + s] - slab * rows
            out = outs[k].at[s] if joined else outs[k * per + s].at[0]
            out[...] = moved[z]


def side_shapes(atlas, width, start):
    rows, ny = atlas.shape[:2]
    deep = rows + 2 * TSTEPS
    scratch = [pltpu.VMEM((3, ny, deep, LANES), F32)] if start == 0 else []
    scratch += [pltpu.VMEM((deep, ny, width, LANES), F32)] * TSTEPS
    return jax.ShapeDtypeStruct((7, ny, deep, LANES), F32), scratch


def first_side(atlas, vel, halo, levels, coef, width, start):
    done = jax.ShapeDtypeStruct((TSTEPS, atlas.shape[1], width, LANES), BF16)
    weights, scratch = side_shapes(atlas, width, start)
    outs = [done, weights] if start == 0 else [done]
    extra = [] if start == 0 else [coef]
    result = pl.pallas_call(
        functools.partial(first_kernel, width, start),
        out_shape=outs,
        in_specs=[spec(pltpu.VMEM)] * (3 + len(levels) + len(extra)),
        out_specs=[spec(pltpu.VMEM)] * len(outs),
        scratch_shapes=scratch,
        compiler_params=params(28),
        cost_estimate=cost(COST_T),
        name="first_side",
    )(atlas, vel, halo, *levels, *extra)
    return result if start == 0 else (result[0], coef)


def second_side(slots, atlas, vel, halo, levels, done, coef, width, start, peers, per, joined):
    rows, ny = atlas.shape[:2]
    out = jax.ShapeDtypeStruct((per if joined else 1, ny, width, LANES), BF16)
    count = peers if joined else peers * per
    weights, scratch = side_shapes(atlas, width, start)
    outs = [out] * count + ([weights] if start == 0 else [])
    extra = [] if start == 0 else [coef]
    result = pl.pallas_call(
        functools.partial(second_kernel, peers, per, joined, width, start),
        out_shape=outs,
        in_specs=[spec(pl.ANY)] + [spec(pltpu.VMEM)] * (4 + len(levels) + len(extra)),
        out_specs=[spec(pltpu.VMEM)] * len(outs),
        scratch_shapes=[pltpu.VMEM((rows, ny, width, LANES), BF16)]
        + scratch
        + [pltpu.SMEM((rows,), jnp.int32), pltpu.SemaphoreType.DMA],
        compiler_params=params(28),
        cost_estimate=cost(COST_T),
        name="second_side",
    )(slots, atlas, vel, halo, done, *levels, *extra)
    return (result[:count], result[count]) if start == 0 else (result, coef)


def dot(a, b):
    return jnp.dot(a, b, preferred_element_type=F32)


def dot_full(a, b):
    return jnp.dot(a, b, preferred_element_type=F32, precision=lax.Precision.HIGHEST)


def halves(value):
    high = value.astype(BF16)
    return high, (value - high.astype(F32)).astype(BF16)


def fit_kernel(parts, peers, mask, density, *refs):
    blocks = refs[: parts * peers]
    outs = refs[parts * peers : parts * peers + peers]
    panel, gram, right, inverse, answer = refs[parts * peers + peers :]
    pixels = panel.shape[1]
    channels = panel.shape[0]
    share = channels // peers
    ny = pixels // LANES
    for k in range(peers):
        first = k * share
        for block in blocks[k * parts : (k + 1) * parts]:
            for y in range(ny):
                rows = slice(first, first + block.shape[2])
                panel[rows, y * LANES : (y + 1) * LANES] = block[0, y]
            first += block.shape[2]
    valid = mask[0] > 0
    every = panel[...]
    maps = density[0]
    masked = jnp.where(valid, every, jnp.zeros_like(every))
    contract = (((1,), (1,)), ((), ()))
    row = lax.broadcasted_iota(jnp.int32, (channels, channels), 0)
    column = lax.broadcasted_iota(jnp.int32, (channels, channels), 1)
    same = row == column
    gram[...] = lax.dot_general(every, masked, contract, preferred_element_type=F32) * (
        1.0 / pixels
    ) + jnp.where(same, RIDGE, 0.0)

    def set_right():
        product = lax.dot_general(maps, masked, contract, preferred_element_type=F32)
        right[...] = product * (1.0 / pixels)

    sums = jnp.sum(jnp.abs(gram[...]), axis=0, keepdims=True)
    bound_row = jnp.max(sums, axis=1, keepdims=True)
    bound = jnp.max(sums)
    start = 2.0 / (RIDGE + bound_row)
    spread = (bound_row - RIDGE) / (bound_row + RIDGE)

    def narrowed(spread):
        square = spread * spread
        return square / (2.0 - square), 2.0 / (2.0 - square)

    def doubled(scale):
        low = inverse[...].astype(BF16)
        left = jnp.where(same, 1.0, 0.0) - dot(gram[...].astype(BF16), low)
        inverse[...] = scale * (inverse[...] + dot(low, left.astype(BF16)))

    def refined():
        high, rest = halves(answer[...])
        gram_high, gram_rest = halves(gram[...])
        product = dot(high, gram_high) + (dot(rest, gram_high) + dot(high, gram_rest))
        left = (right[...] - product).astype(BF16)
        answer[...] = answer[...] + dot(left, inverse[...].astype(BF16))

    def solve(doublings):
        scales = []
        rest = spread
        for _ in range(doublings + 1):
            rest, scale = narrowed(rest)
            scales.append(scale)
        set_right()
        inverse[...] = scales[0] * (
            jnp.where(same, 2.0 * start, 0.0) - (start * start) * gram[...]
        )
        for scale in scales[1:]:
            doubled(scale)
        answer[...] = dot(right[...].astype(BF16), inverse[...].astype(BF16))
        for _ in range(doublings + 1):
            refined()

    @pl.when(bound <= EASY)
    def _():
        solve(1)

    @pl.when((bound > EASY) & (bound <= FAIR))
    def _():
        solve(2)

    @pl.when(bound > FAIR)
    def _():
        set_right()
        inverse[...] = jnp.where(same, start, 0.0)

        def step(spread):
            left = jnp.where(same, 2.0, 0.0) - dot_full(gram[...], inverse[...])
            inverse[...] = dot_full(inverse[...], left)
            return spread * spread

        lax.while_loop(lambda spread: spread > 1e-4, step, jnp.max(spread))
        answer[...] = dot_full(right[...], inverse[...])
        for _ in range(3):
            left = right[...] - dot_full(answer[...], gram[...])
            answer[...] = answer[...] + dot_full(left, inverse[...])

    coefficient_t = answer[...].astype(BF16)
    coefficient = answer[...].T.astype(BF16)
    fitted = dot(coefficient_t, panel[...])
    residual = (fitted - maps.astype(F32)).astype(BF16)
    pushed = dot(coefficient, residual)
    gradient = jnp.where(valid, 2.0 * pushed, 0.0).astype(BF16)
    for k in range(peers):
        for y in range(ny):
            outs[k][y] = gradient[k * share : (k + 1) * share, y * LANES : (y + 1) * LANES]


def fit(mask, density, section, blocks, parts, peers):
    ny = blocks[0].shape[1]
    pixels = ny * LANES
    channels = sum(block.shape[2] for block in blocks)
    classes = density.shape[1]

    def one(block):
        at = section if block.shape[0] > 1 else 0
        return pl.BlockSpec((1,) + block.shape[1:], lambda i: (at, 0, 0, 0))

    out = (ny, channels // peers, LANES)
    return pl.pallas_call(
        functools.partial(fit_kernel, parts, peers),
        grid=(1,),
        out_shape=[jax.ShapeDtypeStruct(out, BF16)] * peers,
        in_specs=[
            pl.BlockSpec((1, 1, pixels), lambda i: (section, 0, 0)),
            pl.BlockSpec((1, classes, pixels), lambda i: (section, 0, 0)),
        ]
        + [one(block) for block in blocks],
        out_specs=[pl.BlockSpec(out, lambda i: (0, 0, 0))] * peers,
        scratch_shapes=[
            pltpu.VMEM((channels, pixels), BF16),
            pltpu.VMEM((channels, channels), F32),
            pltpu.VMEM((classes, channels), F32),
            pltpu.VMEM((channels, channels), F32),
            pltpu.VMEM((classes, channels), F32),
        ],
        compiler_params=params(24),
        cost_estimate=cost(COST_F),
        name="fit",
    )(mask, density, *blocks)


def place_kernel(per, which, slots, *refs):
    blocks, (out, sems) = refs[: len(which)], refs[-2:]
    me = lax.axis_index(("gy", "af"))
    first = lax.axis_index("gz") * out.shape[0]
    copies = []
    for i, (k, section) in enumerate(which):
        z = slots[(me ^ k) * per + section] - first
        copies.append(pltpu.make_async_copy(blocks[i], out.at[z], sems.at[i]))
    for copy in copies:
        copy.start()
    for copy in copies:
        copy.wait()


def place(slots, returned, which, earlier, rows, per):
    blocks = [returned[key] for key in which]
    extra = [] if earlier is None else [earlier]
    return pl.pallas_call(
        functools.partial(place_kernel, per, which),
        out_shape=jax.ShapeDtypeStruct((rows,) + blocks[0].shape, BF16),
        in_specs=[spec(pltpu.SMEM)]
        + [spec(pltpu.VMEM)] * len(blocks)
        + [spec(pl.ANY)] * len(extra),
        out_specs=spec(pl.ANY),
        scratch_shapes=[pltpu.SemaphoreType.DMA((len(blocks),))],
        input_output_aliases={1 + len(blocks): 0} if extra else {},
        compiler_params=params(8),
        cost_estimate=cost(COST_P),
        name="place",
    )(slots, *blocks, *extra)


def body(atlas_features, velocity, section_density, pixel_mask, section_slice):
    rows, channels = atlas_features.shape[:2]
    slabs = lax.axis_size("gz")
    peers = lax.axis_size(("gy", "af"))
    per = section_density.shape[0]
    widths = WIDTHS if sum(WIDTHS) == channels else (channels,)
    chunks = len(widths)

    atlas = jnp.transpose(atlas_features, (0, 2, 1, 3))
    vel = jnp.transpose(velocity, (0, 2, 1, 3))
    mask = pixel_mask.reshape(per, 1, -1)
    slots = section_slice

    edges = pack(atlas, vel, widths[0], 0)
    ones = [(i, i ^ 1) for i in range(slabs)]
    twos = [(i, i + 1) for i in range(1, slabs - 1, 2)]
    twos += [(j, i) for i, j in twos]
    own, _ = lax.optimization_barrier((atlas, edges[0]))
    levels = inner(own, vel)
    halos = []
    for part in range(chunks):
        if part > 0:
            later, _ = lax.optimization_barrier((atlas, edges[0]))
            edges = pack(later, vel, widths[part], sum(widths[:part]))
        one = lax.ppermute(edges[0], "gz", ones)
        two = lax.ppermute(edges[1], "gz", twos)
        halos.append((one, two))

    def swap(block, k):
        if k == 0:
            return block
        return lax.ppermute(block, ("gy", "af"), [(i, i ^ k) for i in range(peers)])

    arrived = {}
    coef_one = coef_two = None
    start = 0
    for part, width in enumerate(widths):
        joined = part < chunks - 1
        one, two = halos[part]
        if part > 0:
            one, _ = lax.optimization_barrier((one, moved[0]))
        done, coef_one = first_side(atlas, vel, one, levels, coef_one, width, start)
        moved, coef_two = second_side(
            slots, atlas, vel, two, levels, done, coef_two, width, start, peers, per, joined
        )
        start += width
        if part > 0:
            moved, waiting, _ = lax.optimization_barrier(
                (moved, waiting, arrived[0, peers // 2, part - 1])
            )
            waiting = swap(waiting, 1)
            for section in range(per):
                arrived[section, 1, part - 1] = waiting
        for s in range(1 if joined else per):
            for k in reversed(range(peers)):
                block = moved[k if joined else k * per + s]
                if joined and k == 1:
                    waiting = block
                    continue
                block = swap(block, k)
                for section in range(per) if joined else [s]:
                    arrived[section, k, part] = block

    returned = {}
    for s in range(per):
        blocks = [arrived[s, k, part] for k in range(peers) for part in range(chunks)]
        gradients = fit(mask, section_density, s, blocks, chunks, peers)
        for k in range(peers):
            returned[k, s] = swap(gradients[k], k)
    last = per - 1
    early = [key for key in returned if key[1] < last or key[0] < peers // 2]
    late = [(k, last) for k in range(peers // 2, peers - 1)]
    result = place(slots, returned, early, None, rows, per)
    result = place(slots, returned, late, result, rows, per)
    far = peers - 1
    at = (lax.axis_index(("gy", "af")) ^ far) * per + last
    at = lax.dynamic_index_in_dim(slots, at, keepdims=False) - lax.axis_index("gz") * rows
    result = lax.dynamic_update_slice(result, returned[far, last][None], (at, 0, 0, 0))
    return jnp.transpose(result, (0, 2, 1, 3))


def solution(mesh):
    return jax.shard_map(
        body,
        mesh=mesh,
        in_specs=(
            P(("groups", "gz"), ("gy", "af"), None, None),
            P(None, ("groups", "gz"), None, None),
            P(("groups", "gz", "gy", "af"), None, None),
            P(("groups", "gz", "gy", "af"), None),
            P(("groups", "gz")),
        ),
        out_specs=P(("groups", "gz"), ("gy", "af"), None, None),
        check_vma=False,
    )
```

```python
import functools
import itertools

import jax
import jax.numpy as jnp
from jax import lax
from jax.experimental import pallas as pl
from jax.experimental.pallas import tpu as pltpu
from jax.sharding import PartitionSpec as P

TSTEPS = 4
RATE = 0.04
RIDGE = 0.25
LANES = 128
F32 = jnp.float32
BF16 = jnp.bfloat16
VEL_ROWS = 16
WIDTHS = (32, 32)
COST_I, COST_T, COST_F, COST_P = 4 * 10**9, 10**8, 10 * 10**9, 10**8
EASY = 1.08
FAIR = 3.8


def spec(memory_space):
    return pl.BlockSpec(memory_space=memory_space)


def cost(count):
    return pl.CostEstimate(flops=count, bytes_accessed=0, transcendentals=0)


def params(mib):
    return pltpu.CompilerParams(vmem_limit_bytes=mib << 20)


def odd_slab():
    return lax.rem(lax.axis_index("gz"), 2)


def pack_kernel(width, start, atlas, vel, low, high, held, boxes, sems):
    outs = (low, high)
    rows, ny = atlas.shape[:2]
    odd = odd_slab()
    slots = TSTEPS - 1
    copies = []
    count = itertools.count()

    def move(source, target):
        copies.append(pltpu.make_async_copy(source, target, sems.at[next(count)]))
        copies[-1].start()

    if start == 0:
        move(vel, held)
    for side in range(2):
        first = jnp.where(odd == side, rows - TSTEPS, 0)
        for step in range(TSTEPS):
            move(
                atlas.at[first + step, :, pl.ds(start, width), :],
                outs[side].at[:, pl.ds(step * width, width), :],
            )
    if start == 0:
        copies.pop(0).wait()
        speed = held[...].astype(F32)
        filler = jnp.zeros((ny, VEL_ROWS - 3 * slots, LANES), F32)
        edges = []
        for first in (0, rows - slots):
            lines = [speed[k, :, first : first + slots, :] for k in range(3)]
            edges.append(jnp.concatenate(lines + [filler], axis=1))
        for side in range(2):
            boxes[side] = jnp.where(odd == side, edges[1], edges[0]).astype(BF16)
            move(boxes.at[side], outs[side].at[:, pl.ds(TSTEPS * width, VEL_ROWS), :])
    for copy in copies:
        copy.wait()


def pack(atlas, vel, width, start):
    ny = atlas.shape[1]
    rows = TSTEPS * width + (VEL_ROWS if start == 0 else 0)
    return pl.pallas_call(
        functools.partial(pack_kernel, width, start),
        out_shape=[jax.ShapeDtypeStruct((ny, rows, LANES), BF16)] * 2,
        in_specs=[spec(pl.ANY)] * 2,
        out_specs=[spec(pl.ANY)] * 2,
        scratch_shapes=[
            pltpu.VMEM(vel.shape, BF16),
            pltpu.VMEM((2, ny, VEL_ROWS, LANES), BF16),
            pltpu.SemaphoreType.DMA((2 * TSTEPS + 3,)),
        ],
        compiler_params=params(8),
        name="pack_edges",
    )(*(pltpu.with_memory_space_constraint(x, pltpu.HBM) for x in (atlas, vel)))


def set_weights(speed, coef, inside):
    lane = lax.broadcasted_iota(jnp.int32, (1,) + speed.shape[2:], 2)
    for y in range(speed.shape[1]):
        total = jnp.zeros(lane.shape, F32)
        for k in range(3):
            v = speed[k, y : y + 1]
            from_low = jnp.maximum(v, 0.0) + RATE
            from_high = RATE - jnp.minimum(v, 0.0)
            total = total + (from_low + from_high)
            if k == 2:
                from_low = jnp.where(lane == 0, 0.0, from_low)
                from_high = jnp.where(lane == LANES - 1, 0.0, from_high)
            coef[2 * k + 1, y : y + 1] = jnp.where(inside, from_low, 0.0)
            coef[2 * k + 2, y : y + 1] = jnp.where(inside, from_high, 0.0)
        coef[0, y : y + 1] = jnp.where(inside, 1.0 - total, 0.0)


def advance(coef, source, target, z, shift=0):
    at = z - shift
    ny = source.shape[1]
    for y in range(ny):
        weight = [coef[i, y, pl.ds(z, 1), :] for i in range(7)]
        center = source[at, y]
        total = weight[0] * center
        total = total + weight[1] * source[at - 1, y]
        total = total + weight[2] * source[at + 1, y]
        if y > 0:
            total = total + weight[3] * source[at, y - 1]
        if y < ny - 1:
            total = total + weight[4] * source[at, y + 1]
        total = total + weight[5] * pltpu.roll(center, 1, axis=1)
        total = total + weight[6] * pltpu.roll(center, LANES - 1, axis=1)
        target[z, y] = total


def advance_pairs(coef, source, target, pairs, first, shift=0):
    def step(i, carry):
        z = first(i)
        advance(coef, source, target, z, shift)
        advance(coef, source, target, z + 1, shift)
        return carry

    lax.fori_loop(0, pairs, step, 0)


def inner_kernel(atlas, vel, one, two, three, state, speed, coef):
    rows = atlas.shape[0]
    speed[...] = vel[...].astype(F32)
    set_weights(speed, coef, True)

    def load(z, carry):
        state[z] = atlas[z].astype(F32)
        return carry

    lax.fori_loop(0, rows, load, 0)
    levels = (state, one, two, three)
    for step in range(TSTEPS - 1):
        pairs = (rows - 2 * (step + 1)) // 2
        first = step + 1
        advance_pairs(coef, levels[step], levels[step + 1], pairs, lambda i: first + 2 * i)


def inner(atlas, vel):
    level = jax.ShapeDtypeStruct(atlas.shape, F32)
    return pl.pallas_call(
        inner_kernel,
        out_shape=[level] * (TSTEPS - 1),
        in_specs=[spec(pltpu.VMEM)] * 2,
        out_specs=[spec(pltpu.VMEM)] * (TSTEPS - 1),
        scratch_shapes=[
            pltpu.VMEM(atlas.shape, F32),
            pltpu.VMEM(vel.shape, F32),
            pltpu.VMEM((7,) + vel.shape[1:], F32),
        ],
        compiler_params=params(24),
        cost_estimate=cost(COST_I),
        name="inner_steps",
    )(atlas, vel)


def side_weights(high, vel, halo, speed, coef):
    rows, deep = vel.shape[2], coef.shape[2]
    edge = TSTEPS - 1
    slab, slabs = lax.axis_index("gz"), lax.axis_size("gz")
    has = jnp.where(high, slab < slabs - 1, slab > 0)
    beyond = halo[:, halo.shape[1] - VEL_ROWS :, :].astype(F32)
    for k in range(3):
        lines = beyond[:, edge * k : edge * (k + 1), :]
        speed[k, :, TSTEPS : TSTEPS + rows, :] = vel[k].astype(F32)
        speed[k, :, 1:TSTEPS, :] = lines
        speed[k, :, TSTEPS + rows : TSTEPS + rows + edge, :] = lines
    place = lax.broadcasted_iota(jnp.int32, (1, deep, LANES), 1)
    inside = ((place >= TSTEPS) & (place < TSTEPS + rows)) | has
    set_weights(speed, coef, inside & (place > 0) & (place < deep - 1))


def side_steps(high, width, start, atlas, halo, levels, state, coef):
    rows = atlas.shape[0]
    deep = rows + 2 * TSTEPS
    channels = slice(start, start + width)
    base = jnp.where(high, TSTEPS + rows, 0)
    for step in range(TSTEPS):
        state[0][base + step] = halo[:, step * width : (step + 1) * width, :].astype(F32)
    for i in range(2):
        z = jnp.where(high, rows - 2, 0) + i
        state[0][z + TSTEPS] = atlas[z, :, channels, :].astype(F32)
        for level in range(1, TSTEPS):
            z = jnp.where(high, rows - 2 - level, level) + i
            state[level][z + TSTEPS] = levels[level - 1][z, :, channels, :]
    for step in range(TSTEPS):
        first = jnp.where(high, deep - 5 - step, step + 1)
        target = state[(step + 1) % TSTEPS]
        for i in range(TSTEPS):
            advance(coef, state[step], target, first + i)


def first_kernel(width, start, atlas, vel, halo, *refs):
    levels, refs = refs[: TSTEPS - 1], refs[TSTEPS - 1 :]
    refs, state = refs[:-TSTEPS], refs[-TSTEPS:]
    high = odd_slab() == 0
    if start == 0:
        done, coef, speed = refs
        side_weights(high, vel, halo, speed, coef)
    else:
        coef, done = refs
    side_steps(high, width, start, atlas, halo, levels, state, coef)
    first = jnp.where(high, atlas.shape[0] - TSTEPS, 0)
    for i in range(TSTEPS):
        done[i] = state[0][first + TSTEPS + i].astype(BF16)


def second_kernel(peers, per, joined, width, start, slots, atlas, vel, halo, done, *refs):
    levels, refs, (order, sem) = refs[: TSTEPS - 1], refs[TSTEPS - 1 : -2], refs[-2:]
    refs, state = refs[:-TSTEPS], refs[-TSTEPS:]
    fetch = pltpu.make_async_copy(slots, order, sem)
    fetch.start()
    high = odd_slab() > 0
    if start == 0:
        outs, (coef, moved, speed) = refs[:-3], refs[-3:]
        side_weights(high, vel, halo, speed, coef)
    else:
        coef, outs, moved = refs[0], refs[1:-1], refs[-1]
    rows, ny = atlas.shape[:2]
    side_steps(high, width, start, atlas, halo, levels, state, coef)
    if rows > 2 * TSTEPS:
        source = levels[-1].at[:, :, start : start + width, :]
        pairs = (rows - 2 * TSTEPS) // 2
        advance_pairs(coef, source, state[0], pairs, lambda i: 2 * TSTEPS + 2 * i, TSTEPS)
        for z in range(TSTEPS, rows - TSTEPS):
            moved[z] = state[0][z + TSTEPS].astype(BF16)
    first = jnp.where(high, rows - TSTEPS, 0)
    other = rows - TSTEPS - first
    for i in range(TSTEPS):
        moved[first + i] = state[0][first + TSTEPS + i].astype(BF16)
        moved[other + i] = done[i]
    me = lax.axis_index(("gy", "af"))
    slab = lax.axis_index("gz")
    fetch.wait()
    for k in range(peers):
        for s in range(per):
            z = order[(me ^ k) * per + s] - slab * rows
            out = outs[k].at[s] if joined else outs[k * per + s].at[0]
            out[...] = moved[z]


def side_shapes(atlas, width, start):
    rows, ny = atlas.shape[:2]
    deep = rows + 2 * TSTEPS
    scratch = [pltpu.VMEM((3, ny, deep, LANES), F32)] if start == 0 else []
    scratch += [pltpu.VMEM((deep, ny, width, LANES), F32)] * TSTEPS
    return jax.ShapeDtypeStruct((7, ny, deep, LANES), F32), scratch


def first_side(atlas, vel, halo, levels, coef, width, start):
    done = jax.ShapeDtypeStruct((TSTEPS, atlas.shape[1], width, LANES), BF16)
    weights, scratch = side_shapes(atlas, width, start)
    outs = [done, weights] if start == 0 else [done]
    extra = [] if start == 0 else [coef]
    result = pl.pallas_call(
        functools.partial(first_kernel, width, start),
        out_shape=outs,
        in_specs=[spec(pltpu.VMEM)] * (3 + len(levels) + len(extra)),
        out_specs=[spec(pltpu.VMEM)] * len(outs),
        scratch_shapes=scratch,
        compiler_params=params(28),
        cost_estimate=cost(COST_T),
        name="first_side",
    )(atlas, vel, halo, *levels, *extra)
    return result if start == 0 else (result[0], coef)


def second_side(slots, atlas, vel, halo, levels, done, coef, width, start, peers, per, joined):
    rows, ny = atlas.shape[:2]
    out = jax.ShapeDtypeStruct((per if joined else 1, ny, width, LANES), BF16)
    count = peers if joined else peers * per
    weights, scratch = side_shapes(atlas, width, start)
    outs = [out] * count + ([weights] if start == 0 else [])
    extra = [] if start == 0 else [coef]
    result = pl.pallas_call(
        functools.partial(second_kernel, peers, per, joined, width, start),
        out_shape=outs,
        in_specs=[spec(pl.ANY)] + [spec(pltpu.VMEM)] * (4 + len(levels) + len(extra)),
        out_specs=[spec(pltpu.VMEM)] * len(outs),
        scratch_shapes=[pltpu.VMEM((rows, ny, width, LANES), BF16)]
        + scratch
        + [pltpu.SMEM((rows,), jnp.int32), pltpu.SemaphoreType.DMA],
        compiler_params=params(28),
        cost_estimate=cost(COST_T),
        name="second_side",
    )(slots, atlas, vel, halo, done, *levels, *extra)
    return (result[:count], result[count]) if start == 0 else (result, coef)


def dot(a, b):
    return jnp.dot(a, b, preferred_element_type=F32)


def dot_full(a, b):
    return jnp.dot(a, b, preferred_element_type=F32, precision=lax.Precision.HIGHEST)


def halves(value):
    high = value.astype(BF16)
    return high, (value - high.astype(F32)).astype(BF16)


def fit_kernel(parts, peers, mask, density, *refs):
    blocks = refs[: parts * peers]
    outs = refs[parts * peers : parts * peers + peers]
    panel, gram, right, inverse, answer = refs[parts * peers + peers :]
    pixels = panel.shape[1]
    channels = panel.shape[0]
    share = channels // peers
    ny = pixels // LANES
    for k in range(peers):
        first = k * share
        for block in blocks[k * parts : (k + 1) * parts]:
            for y in range(ny):
                rows = slice(first, first + block.shape[2])
                panel[rows, y * LANES : (y + 1) * LANES] = block[0, y]
            first += block.shape[2]
    valid = mask[0] > 0
    every = panel[...]
    maps = density[0]
    masked = jnp.where(valid, every, jnp.zeros_like(every))
    contract = (((1,), (1,)), ((), ()))
    row = lax.broadcasted_iota(jnp.int32, (channels, channels), 0)
    column = lax.broadcasted_iota(jnp.int32, (channels, channels), 1)
    same = row == column
    gram[...] = lax.dot_general(every, masked, contract, preferred_element_type=F32) * (
        1.0 / pixels
    ) + jnp.where(same, RIDGE, 0.0)

    def set_right():
        product = lax.dot_general(maps, masked, contract, preferred_element_type=F32)
        right[...] = product * (1.0 / pixels)

    sums = jnp.sum(jnp.abs(gram[...]), axis=0, keepdims=True)
    bound_row = jnp.max(sums, axis=1, keepdims=True)
    bound = jnp.max(sums)
    start = 2.0 / (RIDGE + bound_row)
    spread = (bound_row - RIDGE) / (bound_row + RIDGE)

    def narrowed(spread):
        square = spread * spread
        return square / (2.0 - square), 2.0 / (2.0 - square)

    def doubled(scale):
        low = inverse[...].astype(BF16)
        left = jnp.where(same, 1.0, 0.0) - dot(gram[...].astype(BF16), low)
        inverse[...] = scale * (inverse[...] + dot(low, left.astype(BF16)))

    def refined():
        high, rest = halves(answer[...])
        gram_high, gram_rest = halves(gram[...])
        product = dot(high, gram_high) + (dot(rest, gram_high) + dot(high, gram_rest))
        left = (right[...] - product).astype(BF16)
        answer[...] = answer[...] + dot(left, inverse[...].astype(BF16))

    def solve(doublings):
        scales = []
        rest = spread
        for _ in range(doublings + 1):
            rest, scale = narrowed(rest)
            scales.append(scale)
        set_right()
        inverse[...] = scales[0] * (
            jnp.where(same, 2.0 * start, 0.0) - (start * start) * gram[...]
        )
        for scale in scales[1:]:
            doubled(scale)
        answer[...] = dot(right[...].astype(BF16), inverse[...].astype(BF16))
        for _ in range(doublings + 1):
            refined()

    @pl.when(bound <= EASY)
    def _():
        solve(1)

    @pl.when((bound > EASY) & (bound <= FAIR))
    def _():
        solve(2)

    @pl.when(bound > FAIR)
    def _():
        set_right()
        inverse[...] = jnp.where(same, start, 0.0)

        def step(spread):
            left = jnp.where(same, 2.0, 0.0) - dot_full(gram[...], inverse[...])
            inverse[...] = dot_full(inverse[...], left)
            return spread * spread

        lax.while_loop(lambda spread: spread > 1e-4, step, jnp.max(spread))
        answer[...] = dot_full(right[...], inverse[...])
        for _ in range(3):
            left = right[...] - dot_full(answer[...], gram[...])
            answer[...] = answer[...] + dot_full(left, inverse[...])

    coefficient_t = answer[...].astype(BF16)
    coefficient = answer[...].T.astype(BF16)
    fitted = dot(coefficient_t, panel[...])
    residual = (fitted - maps.astype(F32)).astype(BF16)
    pushed = dot(coefficient, residual)
    gradient = jnp.where(valid, 2.0 * pushed, 0.0).astype(BF16)
    for k in range(peers):
        for y in range(ny):
            outs[k][y] = gradient[k * share : (k + 1) * share, y * LANES : (y + 1) * LANES]


def fit(mask, density, section, blocks, parts, peers):
    ny = blocks[0].shape[1]
    pixels = ny * LANES
    channels = sum(block.shape[2] for block in blocks)
    classes = density.shape[1]

    def one(block):
        at = section if block.shape[0] > 1 else 0
        return pl.BlockSpec((1,) + block.shape[1:], lambda i: (at, 0, 0, 0))

    out = (ny, channels // peers, LANES)
    return pl.pallas_call(
        functools.partial(fit_kernel, parts, peers),
        grid=(1,),
        out_shape=[jax.ShapeDtypeStruct(out, BF16)] * peers,
        in_specs=[
            pl.BlockSpec((1, 1, pixels), lambda i: (section, 0, 0)),
            pl.BlockSpec((1, classes, pixels), lambda i: (section, 0, 0)),
        ]
        + [one(block) for block in blocks],
        out_specs=[pl.BlockSpec(out, lambda i: (0, 0, 0))] * peers,
        scratch_shapes=[
            pltpu.VMEM((channels, pixels), BF16),
            pltpu.VMEM((channels, channels), F32),
            pltpu.VMEM((classes, channels), F32),
            pltpu.VMEM((channels, channels), F32),
            pltpu.VMEM((classes, channels), F32),
        ],
        compiler_params=params(24),
        cost_estimate=cost(COST_F),
        name="fit",
    )(mask, density, *blocks)


def place_kernel(per, which, slots, *refs):
    blocks, (out, sems) = refs[: len(which)], refs[-2:]
    me = lax.axis_index(("gy", "af"))
    first = lax.axis_index("gz") * out.shape[0]
    copies = []
    for i, (k, section) in enumerate(which):
        z = slots[(me ^ k) * per + section] - first
        copies.append(pltpu.make_async_copy(blocks[i], out.at[z], sems.at[i]))
    for copy in copies:
        copy.start()
    for copy in copies:
        copy.wait()


def place(slots, returned, which, earlier, rows, per):
    blocks = [returned[key] for key in which]
    extra = [] if earlier is None else [earlier]
    return pl.pallas_call(
        functools.partial(place_kernel, per, which),
        out_shape=jax.ShapeDtypeStruct((rows,) + blocks[0].shape, BF16),
        in_specs=[spec(pltpu.SMEM)]
        + [spec(pltpu.VMEM)] * len(blocks)
        + [spec(pl.ANY)] * len(extra),
        out_specs=spec(pl.ANY),
        scratch_shapes=[pltpu.SemaphoreType.DMA((len(blocks),))],
        input_output_aliases={1 + len(blocks): 0} if extra else {},
        compiler_params=params(8),
        cost_estimate=cost(COST_P),
        name="place",
    )(slots, *blocks, *extra)


def body(atlas_features, velocity, section_density, pixel_mask, section_slice):
    rows, channels = atlas_features.shape[:2]
    slabs = lax.axis_size("gz")
    peers = lax.axis_size(("gy", "af"))
    per = section_density.shape[0]
    widths = WIDTHS if sum(WIDTHS) == channels else (channels,)
    chunks = len(widths)

    atlas = jnp.transpose(atlas_features, (0, 2, 1, 3))
    vel = jnp.transpose(velocity, (0, 2, 1, 3))
    mask = pixel_mask.reshape(per, 1, -1)
    slots = section_slice

    edges = pack(atlas, vel, widths[0], 0)
    ones = [(i, i ^ 1) for i in range(slabs)]
    twos = [(i, i + 1) for i in range(1, slabs - 1, 2)]
    twos += [(j, i) for i, j in twos]
    own, _ = lax.optimization_barrier((atlas, edges[0]))
    levels = inner(own, vel)
    halos = []
    for part in range(chunks):
        if part > 0:
            later, _ = lax.optimization_barrier((atlas, edges[0]))
            edges = pack(later, vel, widths[part], sum(widths[:part]))
        one = lax.ppermute(edges[0], "gz", ones)
        two = lax.ppermute(edges[1], "gz", twos)
        halos.append((one, two))

    def swap(block, k):
        if k == 0:
            return block
        return lax.ppermute(block, ("gy", "af"), [(i, i ^ k) for i in range(peers)])

    arrived = {}
    coef_one = coef_two = None
    start = 0
    for part, width in enumerate(widths):
        joined = part < chunks - 1
        one, two = halos[part]
        if part > 0:
            one, _ = lax.optimization_barrier((one, moved[0]))
        done, coef_one = first_side(atlas, vel, one, levels, coef_one, width, start)
        moved, coef_two = second_side(
            slots, atlas, vel, two, levels, done, coef_two, width, start, peers, per, joined
        )
        start += width
        if part > 0:
            moved, _ = lax.optimization_barrier((moved, arrived[0, peers // 2, part - 1]))
        for s in range(1 if joined else per):
            for k in reversed(range(peers)):
                block = moved[k if joined else k * per + s]
                block = swap(block, k)
                for section in range(per) if joined else [s]:
                    arrived[section, k, part] = block

    returned = {}
    for s in range(per):
        blocks = [arrived[s, k, part] for k in range(peers) for part in range(chunks)]
        gradients = fit(mask, section_density, s, blocks, chunks, peers)
        for k in range(peers):
            returned[k, s] = swap(gradients[k], k)
    last = per - 1
    early = [key for key in returned if key[1] < last or key[0] < peers // 2]
    late = [(k, last) for k in range(peers // 2, peers - 1)]
    result = place(slots, returned, early, None, rows, per)
    result = place(slots, returned, late, result, rows, per)
    far = peers - 1
    at = (lax.axis_index(("gy", "af")) ^ far) * per + last
    at = lax.dynamic_index_in_dim(slots, at, keepdims=False) - lax.axis_index("gz") * rows
    result = lax.dynamic_update_slice(result, returned[far, last][None], (at, 0, 0, 0))
    return jnp.transpose(result, (0, 2, 1, 3))


def solution(mesh):
    return jax.shard_map(
        body,
        mesh=mesh,
        in_specs=(
            P(("groups", "gz"), ("gy", "af"), None, None),
            P(None, ("groups", "gz"), None, None),
            P(("groups", "gz", "gy", "af"), None, None),
            P(("groups", "gz", "gy", "af"), None),
            P(("groups", "gz")),
        ),
        out_specs=P(("groups", "gz"), ("gy", "af"), None, None),
        check_vma=False,
    )
```
